32 devices in a mesh: dp: 16 (over z, x, core), mp: 2 (over y).
Axes of the slice: x: 2, y: 2, z: 4, core: 2. Of those that a mesh axis runs over, the one named last changes fastest.
Arguments:
- inputs: bfloat16 [32, 3072, 512], P(('dp', 'mp')), may hold values from -6 to 6
- crop_ids: int32 [32, 3072], P('dp'), may hold values from 0 to 3, as said below
- w_heads: bfloat16 [512, 3, 512], P(None, None, 'mp'), may hold values from -0.25 to 0.25
- b_heads: float32 [2, 512], P(None, 'mp'), may hold values from -3 to 3
- w_merge: bfloat16 [512, 512], P('mp'), may hold values from -2 to 2
- b_merge: float32 [512], replicated, may hold values from -3 to 3
- gain_one: float32 [512], replicated, may hold values from 0.5 to 1.5
- shift_one: float32 [512], replicated, may hold values from -2 to 2
- w_expand: bfloat16 [512, 2048], P(None, 'mp'), may hold values from -0.25 to 0.25
- b_expand: float32 [2048], P('mp'), may hold values from -3 to 3
- w_reduce: bfloat16 [2048, 512], P('mp'), may hold values from -0.125 to 0.125
- b_reduce: float32 [512], replicated, may hold values from -3 to 3
- gain_two: float32 [512], replicated, may hold values from 0.5 to 1.5
- shift_two: float32 [512], replicated, may hold values from -2 to 2
- cotangent: bfloat16 [32, 3072, 512], P(('dp', 'mp')), may hold values from -6 to 6
Outputs:
- outputs: bfloat16 [32, 3072, 512], P(('dp', 'mp'))
- grad_inputs: float32 [32, 3072, 512], P(('dp', 'mp'))
- grad_w_heads: float32 [512, 3, 512], P(None, None, 'mp')
- grad_b_heads: float32 [2, 512], P(None, 'mp')
- grad_w_merge: float32 [512, 512], P('mp')
- grad_b_merge: float32 [512], replicated
- grad_gain_one: float32 [512], replicated
- grad_shift_one: float32 [512], replicated
- grad_w_expand: float32 [512, 2048], P(None, 'mp')
- grad_b_expand: float32 [2048], P('mp')
- grad_w_reduce: float32 [2048, 512], P('mp')
- grad_b_reduce: float32 [512], replicated
- grad_gain_two: float32 [512], replicated
- grad_shift_two: float32 [512], replicated
The draws below stay inside these ranges and needn't reach their ends.
Inputs may be any that keep to these rules, and one draw needn't show every extreme that they name: `crop_ids`: along a canvas's raster order its crop ids never fall; a canvas holds at most four crops.
All inputs are finite; a program needn't handle non-finite values.
Results may differ from the reference program's by a relative error of at most 0.028.
Values may be sent and summed in bfloat16 or wider, within the bound.
A program may use at most 320 MiB of HBM per device.

```python
import math
import jax
import jax.numpy as jnp
import numpy as np
from jax import lax

D = 512
H = 8
HD = 64
FF = 2048
CROWS = 32
CCOLS = 96
QROWS = 8
QCOLS = 32
POS = 3072
CANVASES = 32


def draw_crop_ids(key, part):
    key = jax.random.fold_in(key, 7)
    bound_key, whole_key = jax.random.split(key)
    bounds = jax.random.randint(bound_key, (CANVASES, 3), 1, POS)
    chosen = jax.random.randint(whole_key, (), 0, CANVASES)
    canvas_at = jnp.arange(CANVASES)
    bounds = jnp.where((canvas_at == chosen)[:, None], POS, bounds)
    places = jnp.arange(POS)
    counted = (places[None, :, None] >= bounds[:, None, :]).astype(jnp.int32)
    return jnp.sum(counted, axis=2).astype(jnp.int32)


def level_of(own_key, shape, cuts, smallest, top_value):
    def one(axis_at, blocks):
        steps = jax.random.uniform(jax.random.fold_in(jax.random.fold_in(own_key, 6), axis_at), (blocks,), jnp.float32, smallest / len(cuts), top_value / len(cuts))
        return jnp.repeat(jnp.exp(steps), shape[axis_at] // blocks).reshape((-1,) + (1,) * (len(shape) - axis_at - 1))

    level = one(*cuts[0])
    for cut in cuts[1:]:
        level = level * one(*cut)
    return level


def centred(own_key, dims, deviation, limit, cuts=(), dtype=jnp.bfloat16):
    entries = jax.random.normal(own_key, dims, jnp.float32) * deviation
    if len(cuts) > 0:
        entries = level_of(own_key, dims, cuts, -0.22, 0.18) * entries
    return jnp.clip(entries, min=-limit, max=limit).astype(dtype)


def setup_inputs(seed: int = 0) -> dict:
    streams_of = jax.random.split(jax.random.key(seed), 16)
    inputs = centred(streams_of[0], (CANVASES, POS, D), 1.0, 6.0, ((0, 32),))
    crop_ids = draw_crop_ids(jax.random.fold_in(streams_of[15], 71), 0)
    w_heads = centred(streams_of[2], (D, 3, H * HD), D ** -0.5, 0.25, ((2, 2),))
    b_heads = centred(streams_of[3], (2, H * HD), 0.5, 3.0, ((1, 2),), jnp.float32)
    w_merge = centred(streams_of[4], (H * HD, D), (HD // 8) ** -0.5, 2.0, ((0, 2),))
    b_merge = centred(streams_of[5], (D,), 0.5, 3.0, (), jnp.float32)
    gain_one = jnp.clip(1.0 + 0.1 * jax.random.normal(streams_of[6], (D,), jnp.float32), 0.5, 1.5)
    shift_one = centred(streams_of[7], (D,), 0.3, 2.0, (), jnp.float32)
    w_expand = centred(streams_of[8], (D, FF), D ** -0.5, 0.25, ((1, 2),))
    b_expand = centred(streams_of[9], (FF,), 0.5, 3.0, ((0, 2),), jnp.float32)
    w_reduce = centred(streams_of[10], (FF, D), FF ** -0.5, 0.125, ((0, 2),))
    b_reduce = centred(streams_of[11], (D,), 0.5, 3.0, (), jnp.float32)
    gain_two = jnp.clip(1.0 + 0.1 * jax.random.normal(streams_of[12], (D,), jnp.float32), 0.5, 1.5)
    shift_two = centred(streams_of[13], (D,), 0.3, 2.0, (), jnp.float32)
    cotangent = centred(streams_of[14], (CANVASES, POS, D), 1.0, 6.0, ((0, 32),))
    return dict(inputs=inputs, crop_ids=crop_ids, w_heads=w_heads, b_heads=b_heads, w_merge=w_merge, b_merge=b_merge, gain_one=gain_one, shift_one=shift_one, w_expand=w_expand, b_expand=b_expand, w_reduce=w_reduce, b_reduce=b_reduce, gain_two=gain_two, shift_two=shift_two, cotangent=cotangent)


highest = lax.Precision.HIGHEST

@jax.custom_vjp
def low(v):
    return lax.optimization_barrier(v.astype(jnp.bfloat16)).astype(jnp.float32)

@jax.custom_vjp
def low_back(v):
    return v

def low_keep(v):
    return (low(v), None)

def low_pass(kept, grad):
    return (grad,)

def back_keep(v):
    return (v, None)

def back_low(kept, grad):
    return (low(grad),)
low.defvjp(low_keep, low_pass)
low_back.defvjp(back_keep, back_low)

def geometry():
    across = CCOLS // QCOLS
    blocks = CROWS // QROWS * across
    order = np.arange(blocks)
    block_row = order // across * QROWS
    block_col = order % across * QCOLS
    query_at = np.arange(QROWS * QCOLS)
    query_row = block_row[:, None] + query_at[None, :] // QCOLS
    query_col = block_col[:, None] + query_at[None, :] % QCOLS
    key_at = np.arange(4 * QROWS * QCOLS)
    key_row = block_row[:, None] + key_at[None, :] // (2 * QCOLS) - QROWS
    key_col = block_col[:, None] + key_at[None, :] % (2 * QCOLS) - QCOLS // 2
    earlier = key_row[:, None, :] < query_row[:, :, None]
    level = (key_row[:, None, :] == query_row[:, :, None]) & (key_col[:, None, :] <= query_col[:, :, None])
    return jnp.asarray(earlier | level)

def to_blocks(tensor):
    trailing = tensor.shape[1:]
    canvas_grid = tensor.reshape((CROWS // QROWS, QROWS, CCOLS // QCOLS, QCOLS) + trailing)
    canvas_grid = jnp.swapaxes(canvas_grid, 1, 2)
    return canvas_grid.reshape((CROWS // QROWS * (CCOLS // QCOLS), QROWS * QCOLS) + trailing)

def from_blocks(tensor):
    trailing = tensor.shape[2:]
    canvas_grid = tensor.reshape((CROWS // QROWS, CCOLS // QCOLS, QROWS, QCOLS) + trailing)
    canvas_grid = jnp.swapaxes(canvas_grid, 1, 2)
    return canvas_grid.reshape((POS,) + trailing)

def memory(tensor, filler):
    trailing = tensor.shape[1:]
    canvas_grid = tensor.reshape((CROWS, CCOLS) + trailing)
    widths = ((QROWS, 0), (QCOLS // 2, QCOLS // 2)) + ((0, 0),) * len(trailing)
    canvas_grid = jnp.pad(canvas_grid, widths, constant_values=filler)
    across = CCOLS // QCOLS
    pieces = []
    for number in range(CROWS // QROWS * across):
        row_at = number // across * QROWS
        col_at = number % across * QCOLS
        portion = canvas_grid[row_at:row_at + 2 * QROWS, col_at:col_at + 2 * QCOLS]
        pieces.append(portion.reshape((4 * QROWS * QCOLS,) + trailing))
    return jnp.stack(pieces)

def allowed_pairs(labels):
    matching = to_blocks(labels)[:, :, None] == memory(labels, -1)[:, None, :]
    return geometry() & matching

def attend(queries, keys_all, values, labels):
    head_count = queries.shape[1] // HD
    scaling = 1.0 / math.sqrt(HD)
    query_blocks = to_blocks(queries.reshape(POS, head_count, HD))
    key_blocks = memory(keys_all.reshape(POS, head_count, HD), 0.0)
    value_blocks = memory(values.reshape(POS, head_count, HD), 0.0)
    scores = jnp.einsum('bqhe,bkhe->bhqk', query_blocks, key_blocks, precision=highest) * scaling
    scores = low_back(scores)
    masked = jnp.where(allowed_pairs(labels)[:, None], scores, -1000000000.0)
    maximum = lax.optimization_barrier(jnp.max(masked, axis=-1, keepdims=True))
    exponent = jnp.exp(masked - maximum)
    chances = low(exponent / lax.optimization_barrier(jnp.sum(exponent, axis=-1, keepdims=True)))
    combined = jnp.einsum('bhqk,bkhe->bqhe', chances, value_blocks, precision=highest)
    return from_blocks(combined).reshape(POS, head_count * HD)

def layer_norm(tensor, gain_vec, shift_vec):
    centered = tensor - lax.optimization_barrier(jnp.mean(tensor, axis=-1, keepdims=True))
    variance = lax.optimization_barrier(jnp.mean(centered * centered, axis=-1, keepdims=True))
    return centered * lax.rsqrt(variance + 1e-05) * gain_vec + shift_vec

def smooth_gelu(tensor):
    return 0.5 * tensor * (1.0 + jnp.tanh(0.7978845608028654 * (tensor + 0.044715 * tensor * tensor * tensor)))

def forward_layer(params, canvas, labels):
    w_heads, b_heads, w_merge, b_merge, gain_one, shift_one, w_expand, b_expand, w_reduce, b_reduce, gain_two, shift_two = params
    heads_raw = jnp.einsum('pd,dck->cpk', canvas, w_heads, precision=highest)
    zeroes = jnp.zeros_like(b_heads[0])
    heads_raw = heads_raw + jnp.stack([b_heads[0], zeroes, b_heads[1]])[:, None, :]
    rounded = low_back(low(heads_raw))
    attended = low_back(low(attend(rounded[0], rounded[1], rounded[2], labels)))
    branch_one = low_back(jnp.dot(attended, w_merge, precision=highest))
    normed_one = layer_norm(canvas + branch_one + b_merge, gain_one, shift_one)
    hidden_pre = low_back(jnp.dot(low(normed_one), w_expand, precision=highest) + b_expand)
    hidden = low(smooth_gelu(hidden_pre))
    branch_two = low_back(jnp.dot(hidden, w_reduce, precision=highest))
    return layer_norm(normed_one + branch_two + b_reduce, gain_two, shift_two)

def reference(inputs, crop_ids, w_heads, b_heads, w_merge, b_merge, gain_one, shift_one, w_expand, b_expand, w_reduce, b_reduce, gain_two, shift_two, cotangent):
    params = tuple((weight.astype(jnp.float32) for weight in (w_heads, b_heads, w_merge, b_merge, gain_one, shift_one, w_expand, b_expand, w_reduce, b_reduce, gain_two, shift_two)))

    def advance(running, slices):
        canvas, labels, grad_out = slices

        def forward(params_in, canvas_in):
            return forward_layer(params_in, canvas_in, labels)
        result, pullback = jax.vjp(forward, params, canvas)
        grads_params, grad_canvas = pullback(grad_out)
        running = jax.tree.map(jnp.add, running, grads_params)
        return (running, (result.astype(jnp.bfloat16), grad_canvas))
    zeroes = jax.tree.map(jnp.zeros_like, params)
    summed, stacked = lax.scan(advance, zeroes, (inputs.astype(jnp.float32), crop_ids, cotangent.astype(jnp.float32)))
    return (stacked[0], stacked[1], summed[0], summed[1], summed[2], summed[3], summed[4], summed[5], summed[6], summed[7], summed[8], summed[9], summed[10], summed[11])
```

```python
import functools

import jax
import jax.numpy as jnp
from jax import lax
from jax.experimental import pallas as pl
from jax.experimental.pallas import tpu as pltpu
from jax.sharding import PartitionSpec as P

D = 512
FF = 2048
HD = 64
CROWS = 32
CCOLS = 96
QROWS = 8
QCOLS = 32
POS = 3072
QB = QROWS * QCOLS
PAIR = 2 * HD
BIG = 1e30
LOG2E = 1.4426950408889634
HALF = QROWS // 2
LATE = 2 * HALF * QCOLS
AT_EARLY = (0, 12 * 48, 12 * (48 + 64))
AT_LATE = (0, 16 * 48, 16 * (48 + 64))
ROWS_EARLY, ROWS_LATE = 12 * 160, 16 * 160
MIB = 1 << 20
COLS = ((0, 0, 48), (32, 16, 64), (64, 48, 48))
GC = 0.7978845608028654
GA = 0.044715

f32 = jnp.float32
bf16 = jnp.bfloat16


def dot(a, b):
    return lax.dot_general(a, b, (((1,), (0,)), ((), ())), preferred_element_type=f32)


def dot_nt(a, b):
    return lax.dot_general(a, b, (((1,), (1,)), ((), ())), preferred_element_type=f32)


def dot_tn(a, b):
    return lax.dot_general(a, b, (((0,), (0,)), ((), ())), preferred_element_type=f32)


def sliced(function, step, *arrays):
    results = [
        function(*(array[at : at + step] for array in arrays)) for at in range(0, arrays[0].shape[0], step)
    ]
    if isinstance(results[0], tuple):
        return tuple(jnp.concatenate(parts, axis=0) for parts in zip(*results))
    return jnp.concatenate(results, axis=0)


def lanes_of(value):
    return lax.broadcasted_iota(jnp.int32, value.shape, value.ndim - 1)


def lane_row(first, count, scale=1.0):
    lane = lax.broadcasted_iota(jnp.int32, (1, PAIR), 1)
    return jnp.where((lane >= first) & (lane < first + count), scale, 0.0).astype(bf16)


def own_lanes(value, head, scale=1.0):
    return value * lane_row(head * HD, HD, scale)


def stacked(first, second):
    half = first.shape[0] // 2
    return jnp.concatenate([first[:half], second[:half], first[half:], second[half:]], axis=0)


def key_rows(i):
    if isinstance(i, int):
        return slice(max(i - 1, 0) * QROWS, (i + 1) * QROWS)
    return pl.ds(pl.multiple_of(i * QROWS - QROWS, QROWS), 2 * QROWS)


def query_rows(i):
    return pl.ds(i * QROWS if isinstance(i, int) else pl.multiple_of(i * QROWS, QROWS), QROWS)


def window(ref, i, c0, width):
    keys = ref[key_rows(i), c0 : c0 + width, :]
    return keys.reshape(keys.shape[0] * width, keys.shape[2])


def put_tiles(ref, at, value):
    for k in range(value.shape[1] // PAIR):
        ref[k, at : at + value.shape[0], :] = value[:, k * PAIR : (k + 1) * PAIR]


def get_tiles(ref, at, size):
    return jnp.concatenate([ref[k, at : at + size, :] for k in range(ref.shape[0])], axis=1)


def powers(scores, top):
    return jnp.exp2(((scores - top) * LOG2E).astype(bf16))


def three_parts(value):
    parts = []
    for _ in range(3):
        parts.append(value.astype(bf16).astype(f32))
        value = value - parts[-1]
    return parts


class Weights:
    def __init__(self, sources, targets, send, recv):
        self.sources, self.targets, self.send, self.recv = sources, targets, send, recv
        self.me, self.place = lax.axis_index("dp"), lax.axis_index("mp")
        self.core = lax.rem(self.me, 2)

    def copy(self, source, target, number, to):
        return pltpu.make_async_remote_copy(
            src_ref=source,
            dst_ref=target,
            send_sem=self.send.at[number],
            recv_sem=self.recv.at[number],
            device_id=to,
            device_id_type=pl.DeviceIdType.MESH,
        )

    def meet(self):
        barrier = pltpu.get_barrier_semaphore()
        for to in (self.across(), self.beside()):
            pl.semaphore_signal(barrier, inc=1, device_id=to, device_id_type=pl.DeviceIdType.MESH)
        pl.semaphore_wait(barrier, 2)

    def across(self):
        return self.me, 1 - self.place

    def beside(self):
        return self.me + 1 - 2 * self.core, self.place

    def half(self, ref):
        axis = len(ref.shape) - 2
        size = ref.shape[axis] // 2
        rows = pl.ds(pl.multiple_of(self.core * size, 8), size)
        return ref.at[(slice(None),) * axis + (rows,)]

    def first(self, name):
        source, target = self.sources[name], self.targets[name]
        if name < HEADS:
            return self.copy(source, target, 2 * name, self.across())
        return self.copy(self.half(source), self.half(target), 2 * name, self.across())

    def second(self, name):
        mine = self.half(self.targets[name])
        return self.copy(mine, mine, 2 * name + 1, self.beside())


QV, HIDDEN, HEADS, MERGE, EXPAND, REDUCE = range(6)


def attend_forward_kernel(talks, x_refs, w_ref, qv_ref, hot_ref, others, *refs):
    qkv_ref, att_ref, rate_ref, early_hbm, late_hbm, got = refs[:6]
    bias_ref, w_now, v_now, early_ref, late_ref, *ready_refs, sems, landing, talk = refs[6:]
    pair = pl.program_id(0)
    pairs = pl.num_programs(0)
    if talks:
        weights = Weights([qv_ref, others[0], w_ref, *others[1:]], [*landing, *got[HEADS + 1 :]], *talk)
        w_other, v_other = landing[HEADS], landing[QV]
    else:
        w_other, v_other = others

    @pl.when(pair == 0)
    def _():
        if talks:
            weights.meet()
            for name in (HEADS, QV, HIDDEN):
                weights.first(name).start()
        shape = (HALF, 2 * QCOLS, LATE)
        key_row = lax.broadcasted_iota(jnp.int32, shape, 0)
        key_col = lax.broadcasted_iota(jnp.int32, shape, 1) - QCOLS // 2
        query = lax.broadcasted_iota(jnp.int32, shape, 2) % (HALF * QCOLS)
        row, column = query // QCOLS, query % QCOLS
        later = (key_row > row) | ((key_row == row) & (key_col > column))
        bias_ref[...] = jnp.where(later, -BIG, 0.0).astype(f32)
        w_now[...] = w_ref[...]
        v_now[...] = qv_ref[...]

    @pl.when(pair == 2)
    def _():
        w_now[...] = w_other[...]
        v_now[...] = v_other[...]

    @pl.when(lax.rem(pair, 2) == 0)
    def _():
        spans = [slice(p * PAIR, (p + 1) * PAIR) for p in range(2)]
        full = jnp.concatenate([w_now[k][:, span] for span in spans for k in range(3)], axis=1)
        none = jnp.zeros((1, PAIR), f32)
        biases = jnp.concatenate(
            [part for span in spans for part in (v_now[0:1, span], none, v_now[1:2, span])], axis=1
        )

        @pl.loop(0, CROWS // 8)
        def _(step):
            rows = pl.ds(pl.multiple_of(step * 8, 8), 8)
            part = jnp.concatenate([ref[rows].reshape(8 * CCOLS, PAIR) for ref in x_refs], axis=1)
            qkv = (dot(part, full) + biases).astype(bf16)
            for k in range(6):
                qkv_ref[k // 3, k % 3, rows] = qkv[:, k * PAIR : (k + 1) * PAIR].reshape(8, CCOLS, PAIR)

    queries_ref, keys_ref, values_ref = (qkv_ref.at[lax.rem(pair, 2), part] for part in range(3))

    def copies(half):
        rows = pl.ds(2 * half, 2)
        return [
            pltpu.make_async_copy(early_ref.at[half], early_hbm.at[pair, rows], sems.at[half, 0]),
            pltpu.make_async_copy(late_ref.at[half], late_hbm.at[pair, rows], sems.at[half, 1]),
        ]

    def score(i, j):
        q0, c0, width = COLS[j]
        q_rows = query_rows(i)
        queries = queries_ref[q_rows, q0 : q0 + QCOLS, :].reshape(QB, PAIR)
        hot = hot_ref[q_rows, q0 : q0 + QCOLS, :].reshape(QB, PAIR)
        crops = jnp.where(lanes_of(hot) < 4, (hot.astype(f32) - 1.0) * BIG, 0.0).astype(bf16)
        sides = stacked(*(jnp.concatenate([own_lanes(queries, head, 0.125), crops], axis=1) for head in range(2)))
        keys = jnp.concatenate([window(keys_ref, i, c0, width), window(hot_ref, i, c0, width)], axis=1)
        size = keys.shape[0] - HALF * width
        return dot_nt(keys[:size], sides[:LATE]), dot_nt(keys, sides[LATE:])

    def attend(i, j, *scores):
        q0, c0, width = COLS[j]
        q_rows = query_rows(i)
        values_t = window(values_ref, i, c0, width).T
        values_t = jnp.concatenate([values_t, jnp.ones((16, values_t.shape[1]), bf16)], axis=0)
        bias = bias_ref[:, (0 if j != 0 else 16) : (64 if j != 2 else 48), :].reshape(HALF * width, LATE)
        half = LATE // 2
        outs, rates = [], []
        for k, part in enumerate(scores):
            above = part.shape[0] - HALF * width
            own = part[above:] + bias
            part = jnp.concatenate([part[:above], own], axis=0) if above else own
            chances = powers(part, jnp.max(part, axis=0, keepdims=True))
            ref, at = ((early_ref, AT_EARLY), (late_ref, AT_LATE))[k]
            put_tiles(ref.at[i // 2, lax.rem(i, 2)], at[j], chances)
            summed = dot(values_t[:, : chances.shape[0]], chances)
            rates.append(1.0 / summed[PAIR : PAIR + 1])
            summed = summed[:PAIR] * rates[k]
            outs.append(jnp.concatenate([summed[:HD, :half], summed[HD:, half:]], axis=0).T)
        rate_ref[i * 3 + j, 0:1] = jnp.concatenate(rates, axis=1)
        both = jnp.concatenate(outs, axis=0).astype(bf16)
        att_ref[q_rows, q0 : q0 + QCOLS, :] = both.reshape(QROWS, QCOLS, PAIR)

    def block_row(i, ready, following):
        for j in range(3):
            now = ready
            if j < 2:
                ready = score(i, j + 1)
            else:
                for ref, value in zip(ready_refs, score(following, 0)):
                    ref[...] = value
            attend(i, j, *now)

    def move(half, start):
        for copy in copies(half):
            copy.start() if start else copy.wait()

    @pl.when(pair > 0)
    def _():
        move(0, False)

    block_row(0, score(0, 0), 1)

    @pl.loop(1, CROWS // QROWS)
    def _(i):
        @pl.when((i == 2) & (pair > 0))
        def _():
            move(1, False)

        block_row(i, [ref[...] for ref in ready_refs], jnp.minimum(i + 1, CROWS // QROWS - 1))

        @pl.when(i == 1)
        def _():
            move(0, True)

        if talks:

            @pl.when((i == 2) & (pair == pairs - 1))
            def _():
                weights.first(REDUCE).wait()
                weights.second(REDUCE).start()

    move(1, True)

    @pl.when(pair == pairs - 1)
    def _():
        for half in range(2):
            for copy in copies(half):
                copy.wait()

    if talks:

        @pl.when(pair == 0)
        def _():
            weights.first(HEADS).wait()
            weights.second(HEADS).start()
            for name in (MERGE, EXPAND, REDUCE):
                weights.first(name).start()

        @pl.when(pair == 1)
        def _():
            weights.first(QV).wait()
            weights.first(HIDDEN).wait()
            weights.second(HEADS).wait()

        @pl.when(pair == 2)
        def _():
            for name in (MERGE, EXPAND):
                weights.first(name).wait()
                weights.second(name).start()

        @pl.when(pair == pairs - 1)
        def _():
            for k in range(HEADS + 1):
                got[k][...] = landing[k][...]
            for name in (MERGE, EXPAND, REDUCE):
                weights.second(name).wait()


def column_blocks():
    return [
        pl.BlockSpec((CROWS, CCOLS, PAIR), functools.partial(lambda at, g: (0, 0, at), k), pipeline_mode=pl.Buffered(1))
        for k in range(D // PAIR)
    ]


def attend_forward(x, w, biases, hot, others, talks):
    pairs = D // PAIR
    anywhere = pl.BlockSpec(memory_space=pl.ANY)

    def held(*shape):
        return pl.BlockSpec(shape, lambda g: (0,) * len(shape), pipeline_mode=pl.Buffered(1))

    shape = jax.ShapeDtypeStruct
    if talks:
        got = [shape(array.shape, array.dtype) for array in (biases, others[0], w, *others[1:])]
        small = got[: HEADS + 1]
        got_specs = [held(*array.shape) for array in small] + [anywhere] * (len(others) - 1)
        other_specs = [held(*others[0].shape)] + [anywhere] * (len(others) - 1)
        landing = [pltpu.VMEM(array.shape, array.dtype) for array in small]
        talk = [pltpu.SemaphoreType.DMA((12,)), pltpu.SemaphoreType.DMA((12,))]
        params = pltpu.CompilerParams(vmem_limit_bytes=56 * MIB, collective_id=1, has_side_effects=True)
    else:
        got, got_specs, landing, talk = [], [], [], []
        other_specs = [held(*array.shape) for array in others]
        params = pltpu.CompilerParams(vmem_limit_bytes=56 * MIB)
    return pl.pallas_call(
        functools.partial(attend_forward_kernel, talks),
        grid=(pairs,),
        in_specs=[column_blocks(), held(*w.shape), held(*biases.shape), held(CROWS, CCOLS, PAIR), other_specs],
        out_specs=[
            pl.BlockSpec((2, 3, CROWS, CCOLS, PAIR), lambda g: (g // 2, 0, 0, 0, 0)),
            pl.BlockSpec((CROWS, CCOLS, PAIR), lambda g: (0, 0, g)),
            pl.BlockSpec((None, 12, 8, 2 * LATE), lambda g: (g, 0, 0, 0)),
            anywhere,
            anywhere,
            got_specs,
        ],
        out_shape=[
            shape((pairs, 3, CROWS, CCOLS, PAIR), bf16),
            shape((CROWS, CCOLS, pairs * PAIR), bf16),
            shape((pairs, 12, 8, 2 * LATE), f32),
            shape((pairs, CROWS // QROWS, LATE // PAIR, ROWS_EARLY, PAIR), bf16),
            shape((pairs, CROWS // QROWS, LATE // PAIR, ROWS_LATE, PAIR), bf16),
            got,
        ],
        scratch_shapes=[
            pltpu.VMEM((HALF, 2 * QCOLS, LATE), f32),
            pltpu.VMEM(w.shape, bf16),
            pltpu.VMEM(biases.shape, f32),
            pltpu.VMEM((2, 2, LATE // PAIR, ROWS_EARLY, PAIR), bf16),
            pltpu.VMEM((2, 2, LATE // PAIR, ROWS_LATE, PAIR), bf16),
            pltpu.VMEM((12 * COLS[0][2], LATE), f32),
            pltpu.VMEM((16 * COLS[0][2], LATE), f32),
            pltpu.SemaphoreType.DMA((2, 2)),
            landing,
            talk,
        ],
        compiler_params=params,
        cost_estimate=pl.CostEstimate(flops=24_000_000_000, bytes_accessed=60 * MIB, transcendentals=16_000_000),
        name="attend_forward",
    )([x] * (D // PAIR), w, biases, hot, others)


class Links:
    def __init__(self, send, recv):
        self.me, self.place = lax.axis_index("dp"), lax.axis_index("mp")
        self.send, self.recv, self.used = send, recv, 0

    def across(self):
        return self.me, 1 - self.place

    def numbers(self, count):
        self.used += count
        return self.used - count

    def copy(self, source, target, number, to):
        return pltpu.make_async_remote_copy(
            src_ref=source,
            dst_ref=target,
            send_sem=self.send.at[number],
            recv_sem=self.recv.at[number],
            device_id=to,
            device_id_type=pl.DeviceIdType.MESH,
        )

    def meet(self, others):
        barrier = pltpu.get_barrier_semaphore()
        for other in others:
            pl.semaphore_signal(barrier, inc=1, device_id=other, device_id_type=pl.DeviceIdType.MESH)
        pl.semaphore_wait(barrier, len(others))


class Levels:
    def __init__(self, links, groups):
        self.links, self.groups = links, groups

    def __len__(self):
        return len(self.groups)

    def parts(self, level):
        return 1 << len(self.groups[level])

    def index(self, device, level):
        return lax.rem(device // (1 << self.groups[level][0]), self.parts(level))

    def near(self, level):
        me, found = self.links.me, []
        for k in range(1, self.parts(level)):
            to = me
            for n, b in enumerate(self.groups[level]):
                if k >> n & 1:
                    to = to + (1 << b) * (1 - 2 * lax.rem(me // (1 << b), 2))
            found.append((k - 1, (to, self.links.place)))
        return found

    def owned(self, rows, level):
        start, size = 0, rows
        for k in range(level):
            size //= self.parts(k)
            start = start + self.index(self.links.me, k) * size
        return start, size

    def shares(self, rows, level):
        start, size = self.owned(rows, level)
        size //= self.parts(level)
        away = [start + self.index(to, level) * size for _, (to, _) in self.near(level)]
        return start + self.index(self.links.me, level) * size, away, size


def rows_at(ref, start, size):
    return ref.at[pl.ds(pl.multiple_of(start, 16), size)]


def add_rows(target, first, others, step):
    @pl.loop(0, target.shape[0] // step)
    def _(k):
        rows = pl.ds(pl.multiple_of(k * step, 16), step)
        total = first[rows].astype(f32)
        for other in others:
            total = total + other[rows].astype(f32)
        target[rows] = total.astype(target.dtype)


def add_small(running, arrived):
    terms = [running[...]] + arrived
    while len(terms) > 1:
        terms = [terms[k] + terms[k + 1] for k in range(0, len(terms), 2)]
    running[...] = terms[0]


class FeedSum:
    def __init__(self, links, levels, before, own, other, work, work_other, full, parts, parts_other, part_cross, tiny=None):
        self.links, self.levels, self.before = links, levels, before
        self.sources, self.works, self.full = (own, other), (work, work_other), full
        self.parts, self.part_cross = (parts, parts_other), part_cross
        self.rows = work.shape[0]
        self.tiny = tiny
        downs = [("down", level) for level in range(len(levels))]
        ups = [("up", level) for level in reversed(range(len(levels)))]
        self.stages = downs[:before] + [("cross", 0)] + downs[before:] + ups
        self.last = len(self.stages)
        self.base = [links.numbers(3 * levels.parts(level)) for _, level in self.stages]

    def copies(self, stage):
        links, levels, base = self.links, self.levels, self.base[stage]
        kind, level = self.stages[stage]
        near = levels.near(level)
        if kind == "up":
            mine = rows_at(self.full, *levels.owned(self.rows, level + 1))
            return [links.copy(mine, mine, base + k, to) for k, to in near]
        if kind == "cross":
            near = [(0, links.across())]
            kept = rows_at(self.works[1], *levels.owned(self.rows, self.before))
            made = [links.copy(kept, self.part_cross, base, links.across())]
        else:
            made = self.shared(stage, 1 if level < self.before else 0)
        if self.tiny:
            number = base + 2 * levels.parts(level)
            _, running, arrived = self.tiny
            made += [links.copy(running, arrived.at[stage, k], number + k, to) for k, to in near]
        return made

    def shared(self, stage, side):
        levels, base, level = self.levels, self.base[stage], self.stages[stage][1]
        _, away, size = levels.shares(self.rows, level)
        source = self.sources[side] if level == 0 else self.works[side]
        made = []
        for k, to in levels.near(level):
            number, part = base + side * levels.parts(level) + k, self.parts[side][level].at[k]
            made.append(self.links.copy(rows_at(source, away[k], size), part, number, to))
        return made

    def gather(self, stage, side):
        levels, level = self.levels, self.stages[stage][1]
        kept, _, size = levels.shares(self.rows, level)
        source = rows_at(self.sources[side] if level == 0 else self.works[side], kept, size)
        target = rows_at(self.full if level == len(levels) - 1 else self.works[side], kept, size)
        parts = [self.parts[side][level].at[k] for k, _ in levels.near(level)]
        add_rows(target, source, parts, levels.owned(self.rows, len(levels))[1])

    def finish(self, stage):
        levels = self.levels
        kind, level = self.stages[stage]
        for copy in self.copies(stage):
            copy.wait()
        unit = levels.owned(self.rows, len(levels))[1]
        if kind == "cross":
            mine = rows_at(self.works[0], *levels.owned(self.rows, self.before))
            add_rows(mine, mine, [self.part_cross], unit)
        elif kind == "down":
            self.gather(stage, 1 if level < self.before else 0)
        if self.tiny and kind != "up":
            _, running, arrived = self.tiny
            if kind == "cross":
                running[0:8] += arrived[stage, 0, 0:8]
                running[8:10] += arrived[stage, 0, 10:12]
            else:
                add_small(running, [arrived[stage, k] for k, _ in levels.near(level)])

    def step(self, stage):
        if 2 <= stage <= self.before + 1:
            for copy in self.shared(stage - 2, 0):
                copy.wait()
            self.gather(stage - 2, 0)
        if stage > 0:
            self.finish(stage - 1)
        elif self.tiny:
            self.tiny[1][...] = self.tiny[0][...]
        if stage < self.last:
            for copy in self.copies(stage):
                copy.start()
        if 1 <= stage <= self.before:
            for copy in self.shared(stage - 1, 0):
                copy.start()


class HeadSum:
    def __init__(self, links, levels, away, arrived, work, full, parts, bias_away, bias_arrived, bias, bias_parts):
        self.links, self.levels = links, levels
        self.away, self.arrived, self.work, self.full, self.parts = away, arrived, work, full, parts
        self.bias_away, self.bias_arrived, self.bias, self.bias_parts = bias_away, bias_arrived, bias, bias_parts
        self.rows = work.shape[0]
        self.cross_base = links.numbers(2)
        self.last = 2 * len(levels)
        self.base = [links.numbers(2 * levels.parts(self.level(stage))) for stage in range(self.last)]

    def level(self, stage):
        return min(stage, self.last - 1 - stage)

    def cross(self):
        to = self.links.across()
        return [
            self.links.copy(self.away, self.arrived, self.cross_base, to),
            self.links.copy(self.bias_away, self.bias_arrived, self.cross_base + 1, to),
        ]

    def arriving(self, level, k):
        first, size = 0, self.rows
        for at in range(level):
            size //= self.levels.parts(at)
            first += size * (self.levels.parts(at) - 1)
        size //= self.levels.parts(level)
        return self.parts.at[first + k * size : first + (k + 1) * size]

    def copies(self, stage):
        links, levels, base, level = self.links, self.levels, self.base[stage], self.level(stage)
        near = levels.near(level)
        if stage >= len(levels):
            mine = rows_at(self.full, *levels.owned(self.rows, level + 1))
            return [links.copy(mine, mine, base + k, to) for k, to in near]
        _, away, size = levels.shares(self.rows, level)
        return [
            links.copy(rows_at(self.work, away[k], size), self.arriving(level, k), base + k, to) for k, to in near
        ] + [links.copy(self.bias, self.bias_parts.at[level, k], base + levels.parts(level) + k, to) for k, to in near]

    def step(self, stage):
        levels = self.levels
        unit = levels.owned(self.rows, len(levels))[1]
        for copy in self.cross() if stage == 0 else self.copies(stage - 1):
            copy.wait()
        if stage == 0:
            add_rows(self.work, self.work, [self.arrived], unit)
            self.bias[...] += self.bias_arrived[...]
        elif stage <= len(levels):
            level = stage - 1
            kept, _, size = levels.shares(self.rows, level)
            source = rows_at(self.work, kept, size)
            target = rows_at(self.full, kept, size) if stage == len(levels) else source
            add_rows(target, source, [self.arriving(level, k) for k, _ in levels.near(level)], unit)
            add_small(self.bias, [self.bias_parts[level, k] for k, _ in levels.near(level)])
        if stage < self.last:
            for copy in self.copies(stage):
                copy.start()


def groups_of(dp):
    bits = list(range(dp.bit_length() - 1))
    return [bits[:1], bits[1:2], bits[2:]], [bits[:1], bits[1:]]


PLAN = {
    (0, 1): [("expand", 1), ("reduce", 1)],
    (1, 2): [("reduce", 2), ("expand", 2)],
    (1, 4): [("reduce", 3), (0, "cross")],
    (2, 0): [("expand", 3)],
    (2, 1): [(1, "cross")],
    (2, 2): [("reduce", 4)],
    (2, 3): [("expand", 4)],
    (2, 4): [(0, 0)],
    (3, 0): [("reduce", 5)],
    (3, 1): [(0, 1)],
    (3, 2): [("expand", 5)],
    (3, 3): [("reduce", 6), (0, 2)],
    (3, 4): [(1, 0)],
    (4, 1): [(1, 1), ("expand", 6), ("reduce", 7)],
    (4, 2): [(0, 3)],
    (4, 3): [(1, 2), ("expand", 7)],
    (4, 4): [(0, 4), (1, 3), (1, 4)],
}


def attend_backward_kernel(
    dp, qkv_ref, go_ref, delta_ref, rate_ref, x_hbm, w_hbms, gone_hbm, early_hbm, late_hbm, feeds, merges, tiny_ref,
    gx_hbm, gw_ref, gb_ref, sums_out, gk_ref, gv_ref, gqkv_all, early_ref, late_ref, gx_ref, x_ref, w_ref, sems, talk,
):
    pairs = pl.num_programs(0) - 1
    step = pl.program_id(0)
    pair = lax.rem(step + pairs // 2, pairs)
    if dp:
        expand_out, reduce_out, merge_out, small_out, hidden_out = sums_out
        turned_ref, *talk = talk
        expand, reduce, heads, (small, small_in), (send, recv) = talk
        links = Links(send, recv)
        feed_levels, pair_levels = (Levels(links, groups) for groups in groups_of(dp))
        sums = {
            "expand": FeedSum(links, feed_levels, 1, *feeds[0], *expand, tiny=(tiny_ref, small, small_in)),
            "reduce": FeedSum(links, feed_levels, 2, *feeds[1], *reduce),
        }
        for number in range(2):
            sums[number] = HeadSum(links, pair_levels, *heads[number])

    def act(what, stage):
        if stage == "cross":
            for copy in sums[what].cross():
                copy.start()
        else:
            sums[what].step(stage)
            if what == "expand" and stage == sums[what].last:
                leave["expand"].start()
                small_out[...] = small[0:8]
                hidden_out[...] = jnp.concatenate([small[8:9], small[9:10]], axis=1)
            if what == "reduce" and stage == sums[what].last:
                for at in range(0, FF // 2, D):
                    turned_ref[at : at + D] = sums[what].full[:, at : at + D].T
                leave["reduce"].start()

    def event(at_step, place):
        if not dp or (at_step, place) not in PLAN:
            return

        @pl.when(step == at_step)
        def _():
            for what, stage in PLAN[at_step, place]:
                act(what, stage)

    def stored(of, half):
        rows = pl.ds(2 * half, 2)
        return [
            pltpu.make_async_copy(early_hbm.at[of, rows], early_ref.at[half], sems.at[half, 0]),
            pltpu.make_async_copy(late_hbm.at[of, rows], late_ref.at[half], sems.at[half, 1]),
        ]

    fill = pltpu.make_async_copy(gone_hbm, gx_ref, sems.at[2, 0])
    x_in = [
        pltpu.make_async_copy(x_hbm.at[:, :, pl.ds(k * PAIR, PAIR)], x_ref.at[k], sems.at[3 + k, 0])
        for k in range(D // PAIR)
    ]
    w_in = [pltpu.make_async_copy(w_hbms[k], w_ref.at[k], sems.at[3 + k, 1]) for k in range(2)]
    gx_out = [
        pltpu.make_async_copy(gx_ref.at[pl.ds(k * 8, 8)], gx_hbm.at[pl.ds(k * 8, 8)], sems.at[7 + k, 0])
        for k in range(4)
    ]
    if dp:
        leave = {
            "expand": pltpu.make_async_copy(sums["expand"].full, expand_out, sems.at[7, 1]),
            "reduce": pltpu.make_async_copy(turned_ref, reduce_out, sems.at[8, 1]),
        }

    @pl.when(step == 0)
    def _():
        for copy in [*stored(pair, 0), *x_in, *w_in, fill]:
            copy.start()
        if dp:
            links.meet([links.across()] + [to for level in range(2) for _, to in pair_levels.near(level)])
            for name in ("expand", "reduce"):
                sums[name].step(0)

    def fetch(half):
        if half == 0:
            for copy in stored(pair, 1):
                copy.start()
        else:

            @pl.when(step < pairs - 1)
            def _():
                for copy in stored(lax.rem(step + 1 + pairs // 2, pairs), 0):
                    copy.start()

        for copy in stored(pair, half):
            copy.wait()

    @pl.when(step < pairs)
    def _():
        attend_backward_pair(
            pair, qkv_ref, go_ref, delta_ref, rate_ref, gqkv_all.at[pair], early_ref, late_ref, gk_ref, gv_ref, fetch,
            lambda slot: [event(k, slot) for k in range(4)],
        )
        grad = jnp.concatenate([gqkv_all[pair, part].reshape(POS, PAIR) for part in range(3)], axis=1)

        @pl.when(step == 0)
        def _():
            for copy in x_in:
                copy.wait()

        x_all = jnp.concatenate([x_ref[k].reshape(POS, PAIR) for k in range(D // PAIR)], axis=1)
        grad_weights = dot_tn(grad, x_all).T.astype(bf16)
        grad_bias = jnp.broadcast_to(jnp.sum(grad.astype(f32), axis=0, keepdims=True), (8, 3 * PAIR))
        if not dp:
            gw_ref[...] = grad_weights
            gb_ref[...] = grad_bias
        else:
            for number in range(2):
                one = sums[number]
                for first, ref, small_ref in ((0, one.away, one.bias_away), (2, one.work, one.bias)):

                    @pl.when(step == first + number)
                    def _():
                        ref[:, 0 : 3 * PAIR] = grad_weights
                        small_ref[...] = grad_bias
                        if number == 0:
                            merge = merges[1 if first == 0 else 0]
                            for k in range(2):
                                span = slice(k * (D // 2), (k + 1) * (D // 2))
                                ref[span, 3 * PAIR :] = merge[:, span]

            for k in range(4):
                event(k, 4)

    @pl.when(step == pairs)
    def _():
        for copy in [fill, *w_in]:
            copy.wait()
        weights = jnp.concatenate(
            [
                w_ref[p // 2, part, :, p % 2 * PAIR : (p % 2 + 1) * PAIR]
                for p in range(D // PAIR)
                for part in range(3)
            ],
            axis=1,
        )
        for part in range(4):
            event(4, part)
            rows = slice(part * 8, part * 8 + 8)
            grads = [gqkv_all[p, k, rows].reshape(8 * CCOLS, PAIR) for p in range(D // PAIR) for k in range(3)]
            product = dot_nt(jnp.concatenate(grads, axis=1), weights).reshape(8, CCOLS, D)
            gx_ref[rows] = (gx_ref[rows].astype(f32) + product).astype(bf16)
            gx_out[part].start()
        event(4, 4)
        if dp:
            for number in range(2):
                for part in range(3):
                    lanes = slice(part * PAIR, (part + 1) * PAIR)
                    gw_ref[part, :, number * PAIR : (number + 1) * PAIR] = sums[number].full[:, lanes]
            for k in range(2):
                span = slice(k * (D // 2), (k + 1) * (D // 2))
                merge_out[:, span] = sums[0].full[span, 3 * PAIR :]
            for row, part in enumerate((0, 2)):
                lanes = slice(part * PAIR, (part + 1) * PAIR)
                gb_ref[row : row + 1] = jnp.concatenate([sums[p].bias[0:1, lanes] for p in range(2)], axis=1)
            for copy in leave.values():
                copy.wait()
        for copy in gx_out:
            copy.wait()


def attend_backward_pair(
    pair, qkv_ref, go_ref, delta_ref, rate_ref, gqkv_ref, early_ref, late_ref, gk_ref, gv_ref, fetch, event
):
    gk_ref[...] = jnp.zeros_like(gk_ref)
    gv_ref[...] = jnp.zeros_like(gv_ref)

    def gap(i, j):
        q0, c0, width = COLS[j]
        q_rows = query_rows(i)
        grads = go_ref[q_rows, q0 : q0 + QCOLS, :].reshape(QB, PAIR)
        deltas = delta_ref[q_rows, q0 : q0 + QCOLS, :].reshape(QB, PAIR)
        values = window(qkv_ref.at[2], i, c0, width)
        ones = jnp.broadcast_to(lane_row(0, 24), values.shape)
        values = jnp.concatenate([values, ones], axis=1)
        size = values.shape[0] - HALF * width
        own_grad = stacked(*(own_lanes(grads, head) for head in range(2)))
        own_delta = stacked(*(deltas * lane_row(3 * (2 * pair + head), 3) for head in range(2)))
        sides = jnp.concatenate([own_grad, own_delta], axis=1)
        return dot_nt(values[:size], sides[:LATE]), dot_nt(values, sides[LATE:]), own_grad

    def block(i, j, gaps, gaps_late, own_grad):
        q0, c0, width = COLS[j]
        q_rows = query_rows(i)
        queries = qkv_ref[0, q_rows, q0 : q0 + QCOLS, :].reshape(QB, PAIR)
        own = stacked(*(own_lanes(queries, head, 0.125) for head in range(2)))
        keys = window(qkv_ref.at[1], i, c0, width)
        count = keys.shape[0]
        size = count - HALF * width
        rate = rate_ref[i * 3 + j, 0:1, :].astype(bf16)
        chances = get_tiles(early_ref.at[i // 2, i % 2], AT_EARLY[j], size) * rate[:, :LATE]
        late = get_tiles(late_ref.at[i // 2, i % 2], AT_LATE[j], count) * rate[:, LATE:]
        slopes = chances * gaps.astype(bf16)
        slopes_late = late * gaps_late.astype(bf16)
        both = jnp.concatenate([slopes, slopes_late[:size]], axis=1)
        out = dot_tn(both, keys[:size])
        out_late = out[LATE:] + dot_tn(slopes_late[size:], keys[size:])
        half = LATE // 2
        out = [jnp.where(lanes_of(part[:half]) < HD, part[:half], part[half:]) for part in (out[:LATE], out_late)]
        out = (jnp.concatenate(out, axis=0) * 0.125).astype(bf16)
        gqkv_ref[0, q_rows, q0 : q0 + QCOLS, :] = out.reshape(QROWS, QCOLS, PAIR)
        rows = key_rows(i)
        for ref, early, later, side in ((gk_ref, slopes, slopes_late, own), (gv_ref, chances, late, own_grad)):
            both = jnp.concatenate([early, later[:size]], axis=1)
            part = jnp.concatenate([dot(both, side), dot(later[size:], side[LATE:])], axis=0)
            ref[rows, c0 : c0 + width, :] += part.reshape(-1, width, PAIR)

    order = [(i, j) for i in range(CROWS // QROWS) for j in range(3)]
    ready = gap(*order[0])
    for n, (i, j) in enumerate(order):
        now = ready
        if n + 1 < len(order):
            ready = gap(*order[n + 1])
        if j == 0 and i % 2 == 0:
            fetch(i // 2)
        block(i, j, *now)
        if j == 2:
            event(i)

    gqkv_ref[1] = gk_ref[...].astype(bf16)
    gqkv_ref[2] = gv_ref[...].astype(bf16)


def attend_backward(qkv, grad_att, delta, rate, x, w_halves, grad_one, a_stored, b_stored, feeds, merges, tiny, dp):
    pairs = D // PAIR
    levels, pair_levels = ([1 << len(group) for group in groups] for groups in groups_of(max(dp, 1)))

    def turn(g):
        return lax.rem(jnp.minimum(g, pairs - 1) + pairs // 2, pairs)

    def held(*shape):
        return pl.BlockSpec(shape, lambda g: (0,) * len(shape), pipeline_mode=pl.Buffered(1))

    shape, vmem = jax.ShapeDtypeStruct, pltpu.VMEM
    anywhere = pl.BlockSpec(memory_space=pl.ANY)
    outs = [((CROWS, CCOLS, D), bf16)]
    if dp:
        wide = FF // 2
        feed_specs, merge_specs, tiny_spec = [[held(D, wide)] * 2] * 2, [held(D // 2, D)] * 2, held(16, D)
        sum_outs = [((D, wide), bf16), ((wide, D), bf16), ((D // 2, D), bf16), ((8, D), f32), ((1, wide), f32)]
        sum_specs = [anywhere, anywhere] + [held(*dims) for dims, _ in sum_outs[2:]]
        outs += [((3, D, 2 * PAIR), bf16), ((2, 2 * PAIR), f32)]
        out_specs = [anywhere] + [held(*dims) for dims, _ in outs[1:]]
        copies = 2 * 3 * (2 * sum(levels) + max(levels)) + 2 * (2 + 4 * sum(pair_levels))

        def feed_scratch(before):
            parts, size = [], D
            for level in levels:
                size //= level
                parts.append(vmem((level - 1, size, wide), bf16))
            crossing = D
            for level in levels[:before]:
                crossing //= level
            return [vmem((D, wide), bf16)] * 3 + [parts, parts[:before], vmem((crossing, wide), bf16)]

        talk = [
            vmem((wide, D), bf16),
            feed_scratch(1),
            feed_scratch(2),
            [
                [vmem((D, width), bf16)] * 5
                + [vmem((8, 3 * PAIR), f32)] * 3
                + [vmem((len(pair_levels), max(pair_levels) - 1, 8, 3 * PAIR), f32)]
                for width in (3 * PAIR + D // 2, 3 * PAIR)
            ],
            [vmem((16, D), f32), vmem((len(levels) + 1, max(levels) - 1, 16, D), f32)],
            [pltpu.SemaphoreType.DMA((copies,)), pltpu.SemaphoreType.DMA((copies,))],
        ]
        params = pltpu.CompilerParams(vmem_limit_bytes=63 * MIB, collective_id=0, has_side_effects=True)
    else:
        feeds, merges, tiny, feed_specs, merge_specs, tiny_spec, sum_outs, sum_specs, talk = ([] for _ in range(9))
        outs += [((pairs, D, 3 * PAIR), bf16), ((pairs, 8, 3 * PAIR), f32)]
        out_specs = [
            anywhere,
            pl.BlockSpec((None, D, 3 * PAIR), lambda g: (turn(g), 0, 0)),
            pl.BlockSpec((None, 8, 3 * PAIR), lambda g: (turn(g), 0, 0)),
        ]
        params = pltpu.CompilerParams(vmem_limit_bytes=60 * MIB)
    return pl.pallas_call(
        functools.partial(attend_backward_kernel, dp),
        grid=(pairs + 1,),
        in_specs=[
            pl.BlockSpec((None, 3, CROWS, CCOLS, PAIR), lambda g: (turn(g), 0, 0, 0, 0)),
            pl.BlockSpec((CROWS, CCOLS, PAIR), lambda g: (0, 0, turn(g))),
            held(CROWS, CCOLS, PAIR),
            pl.BlockSpec((None, 12, 8, 2 * LATE), lambda g: (turn(g), 0, 0, 0)),
            anywhere,
            [anywhere] * 2,
            anywhere, anywhere, anywhere,
            feed_specs,
            merge_specs,
            tiny_spec,
        ],
        out_specs=[*out_specs, sum_specs],
        out_shape=[shape(*out) for out in outs] + [[shape(*out) for out in sum_outs]],
        scratch_shapes=[
            vmem((CROWS, CCOLS, PAIR), f32),
            vmem((CROWS, CCOLS, PAIR), f32),
            vmem((pairs, 3, CROWS, CCOLS, PAIR), bf16),
            vmem((2, 2, LATE // PAIR, ROWS_EARLY, PAIR), bf16),
            vmem((2, 2, LATE // PAIR, ROWS_LATE, PAIR), bf16),
            vmem((CROWS, CCOLS, D), bf16),
            vmem((D // PAIR, CROWS, CCOLS, PAIR), bf16),
            vmem((2, 3, D, 2 * PAIR), bf16),
            pltpu.SemaphoreType.DMA((11, 2)),
            talk,
        ],
        compiler_params=params,
        cost_estimate=pl.CostEstimate(flops=50_000_000_000, bytes_accessed=90 * MIB, transcendentals=0),
        name="attend_backward",
    )(qkv, grad_att, delta, rate, x, w_halves, grad_one, a_stored, b_stored, feeds, merges, tiny)


ROWS = 512
CHUNK = 512


def feed_kernel(
    x_ref, ct_ref, att_ref, wm_refs, we_refs, be_refs, wr_refs, vec_refs,
    out_ref, gone_ref, gatt_ref, delta_ref, expand_refs, reduce_refs, merge_refs, tiny_ref,
    hid_ref, slope_ref, gpre_ref, grad_rows_t, acc_m, acc_e, acc_r, acc_be, acc_vec, choose_ref, kind_ref,
):
    step = pl.program_id(0)
    last = pl.num_programs(0) - 1
    slot = lax.rem(step, 2)

    @pl.when(step == 0)
    def _():
        for ref in (hid_ref, grad_rows_t, acc_m, acc_e, acc_r, acc_be, acc_vec):
            ref[...] = jnp.zeros_like(ref)
        lane = lax.broadcasted_iota(jnp.int32, (D, PAIR), 1)
        head = lax.broadcasted_iota(jnp.int32, (D, PAIR), 0) // HD
        choose_ref[...] = jnp.where(head == lane // 3, -1.0, 0.0).astype(bf16)
        kind_ref[...] = jnp.where(lane[0:8] % 3 == lax.broadcasted_iota(jnp.int32, (8, PAIR), 0), 1.0, 0.0)

    b_merge, gain_one, shift_one, b_reduce, gain_two, shift_two = (ref[...] for ref in vec_refs)
    half = D // 2
    chunks = [(side, at) for side in range(2) for at in range(0, FF // 2, CHUNK)]
    spans = [slice(n * CHUNK, (n + 1) * CHUNK) for n in range(len(chunks))]

    def normal(z):
        centred = z - jnp.mean(z, axis=1, keepdims=True)
        rate = lax.rsqrt(jnp.mean(centred * centred, axis=1, keepdims=True) + 1e-5)
        return centred * rate, rate

    def normal_back(grad, normed, rate):
        mean = jnp.mean(grad, axis=1, keepdims=True)
        slant = jnp.mean(grad * normed, axis=1, keepdims=True)
        return rate * (grad - mean - normed * slant)

    def column_sum(z):
        return jnp.sum(z, axis=0, keepdims=True)

    def eights(z):
        return sum(z[at : at + 8] for at in range(0, z.shape[0], 8))


    def weight_reduce(n):
        acc_r[:, spans[n]] += dot(grad_rows_t[...], hid_ref[1 - slot, :, spans[n]])

    def norm_one(x, branch):
        first, rate = normal(x.astype(f32) + b_merge + branch)
        normed = first * gain_one + shift_one
        return first, rate, normed, normed.astype(bf16)

    def norm_two(z, cotangent):
        second, rate = normal(z)
        cotangent = cotangent.astype(f32)
        grad = normal_back(cotangent * gain_two, second, rate)
        out = (second * gain_two + shift_two).astype(bf16)
        return out, grad, grad.astype(bf16), eights(cotangent * second), eights(cotangent), eights(grad)

    def back_one(grad_normed, first, rate):
        grad = normal_back(grad_normed * gain_one, first, rate)
        return grad.astype(bf16), eights(grad_normed * first), eights(grad_normed), eights(grad)

    def gelu(pre):
        square = pre * pre
        bent = jnp.tanh(pre * (GC + (GC * GA) * square))
        lead = 0.5 + 0.5 * bent
        hidden = pre * lead
        slope = lead + (hidden * (1.0 - bent)) * (GC + (3 * GC * GA) * square)
        return hidden.astype(bf16), slope.astype(bf16)

    def back(grad, slope):
        grad = (grad * slope.astype(f32)).astype(bf16)
        return grad, eights(grad.astype(f32))

    def expand(rows_in, n):
        side, at = chunks[n]
        return dot(rows_in, we_refs[side][:, at : at + CHUNK]) + be_refs[side][0:1, at : at + CHUNK]

    def grad_hidden(grad_rows, n):
        side, at = chunks[n]
        return dot_nt(grad_rows, wr_refs[side][at : at + CHUNK, :])

    @pl.when(step == last)
    def _():
        for n in range(len(chunks)):
            weight_reduce(n)
        for side in range(2):
            span = slice(side * (FF // 2), (side + 1) * (FF // 2))
            expand_refs[side][...] = acc_e[:, span].astype(bf16)
            reduce_refs[side][...] = acc_r[:, span].astype(bf16)
            merge_refs[side][...] = acc_m[side * half : (side + 1) * half].astype(bf16)
        tiny_ref[...] = jnp.zeros_like(tiny_ref)
        tiny_ref[0:8] = acc_vec[...]
        for k in range(FF // D):
            tiny_ref[8 + k : 9 + k] = acc_be[:, k * D : (k + 1) * D]

    @pl.when(step < last)
    def _():
        branch_one = dot(att_ref[:, :half], wm_refs[0][...]) + dot(att_ref[:, half:], wm_refs[1][...])
        for n in range(len(chunks) // 2):
            weight_reduce(n)
        first, rate_one, normed_one, rows_in = sliced(norm_one, 32, x_ref[...], branch_one)
        summed_two = normed_one + b_reduce
        ready = expand(rows_in, 0)
        for n, (side, at) in enumerate(chunks):
            now = ready
            if n + 1 < len(chunks):
                ready = expand(rows_in, n + 1)
            hidden, slope = sliced(gelu, 16, now)
            hid_ref[slot, :, spans[n]] = hidden
            slope_ref[:, spans[n]] = slope
            summed_two += dot(hidden, wr_refs[side][at : at + CHUNK, :])
        for n in range(len(chunks) // 2, len(chunks)):
            weight_reduce(n)
        out_ref[...], grad_two, grad_rows, *partial = sliced(norm_two, 32, summed_two, ct_ref[...])
        for k, part in zip((4, 5, 3), partial):
            acc_vec[k : k + 1] += column_sum(part)
        grad_rows_t[...] = grad_rows.T
        grad_normed = grad_two
        ready = grad_hidden(grad_rows, 0)
        for n, (side, at) in enumerate(chunks):
            now = ready
            if n + 1 < len(chunks):
                ready = grad_hidden(grad_rows, n + 1)
            grad_pre, part = sliced(back, 32, now, slope_ref[:, spans[n]])
            gpre_ref[:, spans[n]] = grad_pre
            acc_be[:, spans[n]] += column_sum(part)
            grad_normed += dot_nt(grad_pre, we_refs[side][:, at : at + CHUNK])
        rows_t = rows_in.T
        for n in range(len(chunks)):
            acc_e[:, spans[n]] += dot(rows_t, gpre_ref[:, spans[n]])
        grad_one_rows, *partial = sliced(back_one, 32, grad_normed, first, rate_one)
        gone_ref[...] = grad_one_rows
        for k, part in zip((1, 2, 0), partial):
            acc_vec[k : k + 1] += column_sum(part)
        for side in range(2):
            gatt_ref[:, side * half : (side + 1) * half] = dot_nt(grad_one_rows, wm_refs[side][...]).astype(bf16)
        acc_m[...] += dot(att_ref[...].T, grad_one_rows)
        products = gatt_ref[...].astype(f32) * att_ref[...].astype(f32)
        deltas = three_parts(dot(products.astype(bf16), choose_ref[...]))
        delta_ref[...] = sum(part * kind_ref[k : k + 1] for k, part in enumerate(deltas)).astype(bf16)


def feed(x, cotangent, att, wms, wes, be, wrs, vecs):
    half = D // 2

    def rows(width):
        return pl.BlockSpec((ROWS, width), lambda s: (jnp.minimum(s, POS // ROWS - 1), 0))

    def whole(*shape):
        return pl.BlockSpec(shape, lambda s: (0, 0), pipeline_mode=pl.Buffered(1))

    def held(*shape):
        return pl.BlockSpec(shape, lambda s: (0, 0))

    shape = jax.ShapeDtypeStruct
    return pl.pallas_call(
        feed_kernel,
        grid=(POS // ROWS + 1,),
        in_specs=[
            rows(D), rows(D), rows(D), [whole(half, D)] * 2, [whole(D, FF // 2)] * 2,
            [whole(1, FF // 2)] * 2, [whole(FF // 2, D)] * 2, [whole(1, D)] * 6,
        ],
        out_specs=[
            rows(D), rows(D), rows(D), rows(PAIR), [held(D, FF // 2)] * 2, [held(D, FF // 2)] * 2, [held(half, D)] * 2,
            held(16, D),
        ],
        out_shape=[
            shape((POS, D), bf16), shape((POS, D), bf16), shape((POS, D), bf16), shape((POS, PAIR), bf16),
            [shape((D, FF // 2), bf16)] * 2, [shape((D, FF // 2), bf16)] * 2, [shape((half, D), bf16)] * 2,
            shape((16, D), f32),
        ],
        scratch_shapes=[
            pltpu.VMEM((2, ROWS, FF), bf16),
            pltpu.VMEM((ROWS, FF), bf16),
            pltpu.VMEM((ROWS, FF), bf16),
            pltpu.VMEM((D, ROWS), bf16),
            pltpu.VMEM((D, D), f32),
            pltpu.VMEM((D, FF), f32),
            pltpu.VMEM((D, FF), f32),
            pltpu.VMEM((1, FF), f32),
            pltpu.VMEM((8, D), f32),
            pltpu.VMEM((D, PAIR), bf16),
            pltpu.VMEM((8, PAIR), f32),
        ],
        compiler_params=pltpu.CompilerParams(vmem_limit_bytes=60 * MIB),
        cost_estimate=pl.CostEstimate(flops=44_000_000_000, bytes_accessed=40 * MIB, transcendentals=6_000_000),
        name="feed",
    )(x, cotangent, att, wms, wes, be, wrs, vecs)


def finish_kernel(*refs):
    count = (len(refs) - 5) // 2
    for source, target in zip(refs[: count - 1], refs[count:-6]):
        target[...] = source[...].astype(f32)
    for k, target in enumerate(refs[-6:]):
        target[...] = refs[count - 1][k : k + 1]


def finish(wide, small, vecs):
    def block(array, parts):
        dims = array.shape
        part = dims[:-2] + (dims[-2] // parts, dims[-1])
        return pl.BlockSpec(part, lambda s: (0,) * (len(dims) - 2) + ((s if parts > 1 else 0), 0))

    parts = 2
    specs = [block(array, parts) for array in wide] + [block(array, 1) for array in small]
    row = jax.ShapeDtypeStruct((1, D), f32)
    return pl.pallas_call(
        finish_kernel,
        grid=(parts,),
        in_specs=specs + [block(vecs, 1)],
        out_specs=specs + [block(row, 1)] * 6,
        out_shape=[jax.ShapeDtypeStruct(array.shape, f32) for array in (*wide, *small)] + [row] * 6,
        compiler_params=pltpu.CompilerParams(vmem_limit_bytes=63 * MIB),
        cost_estimate=pl.CostEstimate(flops=0, bytes_accessed=20 * MIB, transcendentals=0),
        name="finish",
    )(*wide, *small, vecs)


def local(
    inputs, crop_ids, w_heads, b_heads, w_merge, b_merge, gain_one, shift_one, w_expand, b_expand, w_reduce,
    b_reduce, gain_two, shift_two, cotangent, *, split,
):
    features = inputs.shape[2]
    dp, mp = split
    paired = mp == 2
    talks = paired and dp >= 8 and dp & (dp - 1) == 0 and D % (16 * dp) == 0
    place = lax.axis_index("mp")

    def both(shard, axis):
        if paired:
            return [shard, lax.ppermute(shard, "mp", [(0, 1), (1, 0)])]
        whole = lax.all_gather(shard, "mp", axis=axis, tiled=True)
        return list(jnp.split(whole, 2, axis=axis))

    def sum_parts(parts, axis):
        if paired:
            arrived = lax.ppermute(parts[1], "mp", [(0, 1), (1, 0)])
            return parts[0].astype(f32) + arrived.astype(f32)
        return lax.psum_scatter(jnp.concatenate(parts, axis=axis), "mp", scatter_dimension=axis, tiled=True)

    canvas = inputs[0].reshape(CROWS, CCOLS, features)
    labels = lax.dynamic_index_in_dim(crop_ids, place, 0, keepdims=False)
    hot = (labels[:, None] == jnp.arange(PAIR)[None, :]).astype(bf16).reshape(CROWS, CCOLS, PAIR)

    own_heads = jnp.transpose(w_heads, (1, 0, 2))
    vecs = [vec[None] for vec in (b_merge, gain_one, shift_one, b_reduce, gain_two, shift_two)]

    if talks:
        qkv, att, rate, a_stored, b_stored, got = attend_forward(
            canvas, own_heads, b_heads, hot, [b_expand[None], w_merge, w_expand, w_reduce], True
        )
        heads, merges = [own_heads, got[HEADS]], [w_merge, got[MERGE]]
        expands, reduces = [w_expand, got[EXPAND]], [w_reduce, got[REDUCE]]
        hiddens = [b_expand[None], got[HIDDEN]]
    else:
        heads, merges, expands, reduces = both(own_heads, 2), both(w_merge, 0), both(w_expand, 1), both(w_reduce, 0)
        biases = [part.astype(f32) for part in both(b_heads.astype(bf16), 1)]
        hiddens = [part[None].astype(f32) for part in both(b_expand.astype(bf16), 0)]
        qkv, att, rate, a_stored, b_stored, _ = attend_forward(
            canvas, heads[0], biases[0], hot, [heads[1], biases[1]], False
        )
    outputs, grad_one, grad_att, delta, expand_g, reduce_g, merge_g, tiny = feed(
        inputs[0], cotangent[0], att.reshape(POS, -1), merges, expands, hiddens, reduces, vecs
    )

    def canvas_of(array):
        return array.reshape(CROWS, CCOLS, -1)

    grad_inputs, heads_g, bias_g, sums = attend_backward(
        qkv, canvas_of(grad_att), canvas_of(delta), rate, canvas, heads, canvas_of(grad_one), a_stored, b_stored,
        [expand_g, reduce_g], merge_g, tiny, dp if talks else 0,
    )

    def bias_part(g_bias):
        g_bias = g_bias[:, 0].reshape(-1, 3, PAIR)
        return jnp.stack([g_bias[:, 0].reshape(-1), g_bias[:, 2].reshape(-1)])

    if talks:
        expand_g, reduce_g, merge_g, tiny_g, be_g = sums
        grad_inputs, expand_g, reduce_g, merge_g, heads_g, be_g, bias_g, *tiny_g = finish(
            [grad_inputs.reshape(POS, D), expand_g, reduce_g, merge_g, heads_g], [be_g, bias_g], tiny_g
        )
        be_g = be_g[0]
        tiny_g = [vec[0] for vec in tiny_g]
    else:
        heads_g = heads_g.reshape(-1, D, 3, PAIR).transpose(2, 1, 0, 3).reshape(3, D, -1)
        grads = (
            (jnp.split(heads_g, 2, axis=2), 2),
            (jnp.split(bias_part(bias_g).astype(bf16), 2, axis=1), 1),
            (expand_g, 1),
            ([half.T for half in reduce_g], 0),
            (merge_g, 0),
            (jnp.split(tiny[8:12].reshape(-1).astype(bf16), 2), 0),
        )
        heads_g, bias_g, expand_g, reduce_g, merge_g, be_g = (
            lax.psum(sum_parts(list(parts), axis).astype(bf16), "dp").astype(f32) for parts, axis in grads
        )
        tiny_g = lax.psum(tiny, ("dp", "mp"))
    return (
        outputs[None],
        grad_inputs.reshape(1, POS, D).astype(f32),
        jnp.transpose(heads_g.astype(f32), (1, 0, 2)),
        bias_g,
        merge_g.astype(f32),
        tiny_g[0],
        tiny_g[1],
        tiny_g[2],
        expand_g.astype(f32),
        be_g,
        reduce_g.astype(f32),
        tiny_g[3],
        tiny_g[4],
        tiny_g[5],
    )


def solution(mesh):
    rows = P(("dp", "mp"), None, None)
    weights = (P(None, None, "mp"), P(None, "mp"), P("mp", None))
    feeds = (P(None, "mp"), P("mp"), P("mp", None))
    return jax.shard_map(
        functools.partial(local, split=(mesh.shape["dp"], mesh.shape["mp"])),
        mesh=mesh,
        in_specs=(rows, P("dp", None), *weights, P(), P(), P(), *feeds, P(), P(), P(), rows),
        out_specs=(rows, rows, *weights, P(), P(), P(), *feeds, P(), P(), P()),
        check_vma=False,
    )
```

```python
import functools

import jax
import jax.numpy as jnp
from jax import lax
from jax.experimental import pallas as pl
from jax.experimental.pallas import tpu as pltpu
from jax.sharding import PartitionSpec as P

D = 512
FF = 2048
HD = 64
CROWS = 32
CCOLS = 96
QROWS = 8
QCOLS = 32
POS = 3072
QB = QROWS * QCOLS
PAIR = 2 * HD
BIG = 1e30
LOG2E = 1.4426950408889634
HALF = QROWS // 2
LATE = 2 * HALF * QCOLS
AT_EARLY = (0, 12 * 48, 12 * (48 + 64))
AT_LATE = (0, 16 * 48, 16 * (48 + 64))
ROWS_EARLY, ROWS_LATE = 12 * 160, 16 * 160
MIB = 1 << 20
COLS = ((0, 0, 48), (32, 16, 64), (64, 48, 48))
GC = 0.7978845608028654
GA = 0.044715

f32 = jnp.float32
bf16 = jnp.bfloat16


def dot(a, b):
    return lax.dot_general(a, b, (((1,), (0,)), ((), ())), preferred_element_type=f32)


def dot_nt(a, b):
    return lax.dot_general(a, b, (((1,), (1,)), ((), ())), preferred_element_type=f32)


def dot_tn(a, b):
    return lax.dot_general(a, b, (((0,), (0,)), ((), ())), preferred_element_type=f32)


def sliced(function, step, *arrays):
    results = [
        function(*(array[at : at + step] for array in arrays)) for at in range(0, arrays[0].shape[0], step)
    ]
    if isinstance(results[0], tuple):
        return tuple(jnp.concatenate(parts, axis=0) for parts in zip(*results))
    return jnp.concatenate(results, axis=0)


def lanes_of(value):
    return lax.broadcasted_iota(jnp.int32, value.shape, value.ndim - 1)


def lane_row(first, count, scale=1.0):
    lane = lax.broadcasted_iota(jnp.int32, (1, PAIR), 1)
    return jnp.where((lane >= first) & (lane < first + count), scale, 0.0).astype(bf16)


def own_lanes(value, head, scale=1.0):
    return value * lane_row(head * HD, HD, scale)


def stacked(first, second):
    half = first.shape[0] // 2
    return jnp.concatenate([first[:half], second[:half], first[half:], second[half:]], axis=0)


def key_rows(i):
    if isinstance(i, int):
        return slice(max(i - 1, 0) * QROWS, (i + 1) * QROWS)
    return pl.ds(pl.multiple_of(i * QROWS - QROWS, QROWS), 2 * QROWS)


def query_rows(i):
    return pl.ds(i * QROWS if isinstance(i, int) else pl.multiple_of(i * QROWS, QROWS), QROWS)


def window(ref, i, c0, width):
    keys = ref[key_rows(i), c0 : c0 + width, :]
    return keys.reshape(keys.shape[0] * width, keys.shape[2])


def put_tiles(ref, at, value):
    for k in range(value.shape[1] // PAIR):
        ref[k, at : at + value.shape[0], :] = value[:, k * PAIR : (k + 1) * PAIR]


def get_tiles(ref, at, size):
    return jnp.concatenate([ref[k, at : at + size, :] for k in range(ref.shape[0])], axis=1)


def powers(scores, top):
    return jnp.exp2(((scores - top) * LOG2E).astype(bf16))


def three_parts(value):
    parts = []
    for _ in range(3):
        parts.append(value.astype(bf16).astype(f32))
        value = value - parts[-1]
    return parts


class Weights:
    def __init__(self, sources, targets, send, recv):
        self.sources, self.targets, self.send, self.recv = sources, targets, send, recv
        self.me, self.place = lax.axis_index("dp"), lax.axis_index("mp")
        self.core = lax.rem(self.me, 2)

    def copy(self, source, target, number, to):
        return pltpu.make_async_remote_copy(
            src_ref=source,
            dst_ref=target,
            send_sem=self.send.at[number],
            recv_sem=self.recv.at[number],
            device_id=to,
            device_id_type=pl.DeviceIdType.MESH,
        )

    def meet(self):
        barrier = pltpu.get_barrier_semaphore()
        for to in (self.across(), self.beside()):
            pl.semaphore_signal(barrier, inc=1, device_id=to, device_id_type=pl.DeviceIdType.MESH)
        pl.semaphore_wait(barrier, 2)

    def across(self):
        return self.me, 1 - self.place

    def beside(self):
        return self.me + 1 - 2 * self.core, self.place

    def half(self, ref):
        axis = len(ref.shape) - 2
        size = ref.shape[axis] // 2
        rows = pl.ds(pl.multiple_of(self.core * size, 8), size)
        return ref.at[(slice(None),) * axis + (rows,)]

    def first(self, name):
        source, target = self.sources[name], self.targets[name]
        if name < HEADS:
            return self.copy(source, target, 2 * name, self.across())
        return self.copy(self.half(source), self.half(target), 2 * name, self.across())

    def second(self, name):
        mine = self.half(self.targets[name])
        return self.copy(mine, mine, 2 * name + 1, self.beside())


QV, HIDDEN, HEADS, MERGE, EXPAND, REDUCE = range(6)


def attend_forward_kernel(talks, x_refs, w_ref, qv_ref, hot_ref, others, *refs):
    qkv_ref, att_ref, rate_ref, early_hbm, late_hbm, got = refs[:6]
    bias_ref, w_now, v_now, early_ref, late_ref, *ready_refs, sems, landing, talk = refs[6:]
    pair = pl.program_id(0)
    pairs = pl.num_programs(0)
    if talks:
        weights = Weights([qv_ref, others[0], w_ref, *others[1:]], [*landing, *got[HEADS + 1 :]], *talk)
        w_other, v_other = landing[HEADS], landing[QV]
    else:
        w_other, v_other = others

    @pl.when(pair == 0)
    def _():
        if talks:
            weights.meet()
            for name in (HEADS, QV, HIDDEN):
                weights.first(name).start()
        shape = (HALF, 2 * QCOLS, LATE)
        key_row = lax.broadcasted_iota(jnp.int32, shape, 0)
        key_col = lax.broadcasted_iota(jnp.int32, shape, 1) - QCOLS // 2
        query = lax.broadcasted_iota(jnp.int32, shape, 2) % (HALF * QCOLS)
        row, column = query // QCOLS, query % QCOLS
        later = (key_row > row) | ((key_row == row) & (key_col > column))
        bias_ref[...] = jnp.where(later, -BIG, 0.0).astype(f32)
        w_now[...] = w_ref[...]
        v_now[...] = qv_ref[...]

    @pl.when(pair == 2)
    def _():
        w_now[...] = w_other[...]
        v_now[...] = v_other[...]

    @pl.when(lax.rem(pair, 2) == 0)
    def _():
        spans = [slice(p * PAIR, (p + 1) * PAIR) for p in range(2)]
        full = jnp.concatenate([w_now[k][:, span] for span in spans for k in range(3)], axis=1)
        none = jnp.zeros((1, PAIR), f32)
        biases = jnp.concatenate(
            [part for span in spans for part in (v_now[0:1, span], none, v_now[1:2, span])], axis=1
        )

        @pl.loop(0, CROWS // 8)
        def _(step):
            rows = pl.ds(pl.multiple_of(step * 8, 8), 8)
            part = jnp.concatenate([ref[rows].reshape(8 * CCOLS, PAIR) for ref in x_refs], axis=1)
            qkv = (dot(part, full) + biases).astype(bf16)
            for k in range(6):
                qkv_ref[k // 3, k % 3, rows] = qkv[:, k * PAIR : (k + 1) * PAIR].reshape(8, CCOLS, PAIR)

    queries_ref, keys_ref, values_ref = (qkv_ref.at[lax.rem(pair, 2), part] for part in range(3))

    def copies(half):
        rows = pl.ds(2 * half, 2)
        return [
            pltpu.make_async_copy(early_ref.at[half], early_hbm.at[pair, rows], sems.at[half, 0]),
            pltpu.make_async_copy(late_ref.at[half], late_hbm.at[pair, rows], sems.at[half, 1]),
        ]

    def score(i, j):
        q0, c0, width = COLS[j]
        q_rows = query_rows(i)
        queries = queries_ref[q_rows, q0 : q0 + QCOLS, :].reshape(QB, PAIR)
        hot = hot_ref[q_rows, q0 : q0 + QCOLS, :].reshape(QB, PAIR)
        crops = jnp.where(lanes_of(hot) < 4, (hot.astype(f32) - 1.0) * BIG, 0.0).astype(bf16)
        sides = stacked(*(jnp.concatenate([own_lanes(queries, head, 0.125), crops], axis=1) for head in range(2)))
        keys = jnp.concatenate([window(keys_ref, i, c0, width), window(hot_ref, i, c0, width)], axis=1)
        size = keys.shape[0] - HALF * width
        return dot_nt(keys[:size], sides[:LATE]), dot_nt(keys, sides[LATE:])

    def attend(i, j, *scores):
        q0, c0, width = COLS[j]
        q_rows = query_rows(i)
        values_t = window(values_ref, i, c0, width).T
        values_t = jnp.concatenate([values_t, jnp.ones((16, values_t.shape[1]), bf16)], axis=0)
        bias = bias_ref[:, (0 if j != 0 else 16) : (64 if j != 2 else 48), :].reshape(HALF * width, LATE)
        half = LATE // 2
        outs, rates = [], []
        for k, part in enumerate(scores):
            above = part.shape[0] - HALF * width
            own = part[above:] + bias
            part = jnp.concatenate([part[:above], own], axis=0) if above else own
            chances = powers(part, jnp.max(part, axis=0, keepdims=True))
            ref, at = ((early_ref, AT_EARLY), (late_ref, AT_LATE))[k]
            put_tiles(ref.at[i // 2, lax.rem(i, 2)], at[j], chances)
            summed = dot(values_t[:, : chances.shape[0]], chances)
            rates.append(1.0 / summed[PAIR : PAIR + 1])
            summed = summed[:PAIR] * rates[k]
            outs.append(jnp.concatenate([summed[:HD, :half], summed[HD:, half:]], axis=0).T)
        rate_ref[i * 3 + j, 0:1] = jnp.concatenate(rates, axis=1)
        both = jnp.concatenate(outs, axis=0).astype(bf16)
        att_ref[q_rows, q0 : q0 + QCOLS, :] = both.reshape(QROWS, QCOLS, PAIR)

    def block_row(i, ready, following):
        for j in range(3):
            now = ready
            if j < 2:
                ready = score(i, j + 1)
            else:
                for ref, value in zip(ready_refs, score(following, 0)):
                    ref[...] = value
            attend(i, j, *now)

    def move(half, start):
        for copy in copies(half):
            copy.start() if start else copy.wait()

    @pl.when(pair > 0)
    def _():
        move(0, False)

    block_row(0, score(0, 0), 1)

    @pl.loop(1, CROWS // QROWS)
    def _(i):
        @pl.when((i == 2) & (pair > 0))
        def _():
            move(1, False)

        block_row(i, [ref[...] for ref in ready_refs], jnp.minimum(i + 1, CROWS // QROWS - 1))

        @pl.when(i == 1)
        def _():
            move(0, True)

        if talks:

            @pl.when((i == 2) & (pair == pairs - 1))
            def _():
                weights.first(REDUCE).wait()
                weights.second(REDUCE).start()

    move(1, True)

    @pl.when(pair == pairs - 1)
    def _():
        for half in range(2):
            for copy in copies(half):
                copy.wait()

    if talks:

        @pl.when(pair == 0)
        def _():
            weights.first(HEADS).wait()
            weights.second(HEADS).start()
            for name in (MERGE, EXPAND, REDUCE):
                weights.first(name).start()

        @pl.when(pair == 1)
        def _():
            weights.first(QV).wait()
            weights.first(HIDDEN).wait()
            weights.second(HEADS).wait()

        @pl.when(pair == 2)
        def _():
            for name in (MERGE, EXPAND):
                weights.first(name).wait()
                weights.second(name).start()

        @pl.when(pair == pairs - 1)
        def _():
            for k in range(HEADS + 1):
                got[k][...] = landing[k][...]
            for name in (MERGE, EXPAND, REDUCE):
                weights.second(name).wait()


def column_blocks():
    return [
        pl.BlockSpec((CROWS, CCOLS, PAIR), functools.partial(lambda at, g: (0, 0, at), k), pipeline_mode=pl.Buffered(1))
        for k in range(D // PAIR)
    ]


def attend_forward(x, w, biases, hot, others, talks):
    pairs = D // PAIR
    anywhere = pl.BlockSpec(memory_space=pl.ANY)

    def held(*shape):
        return pl.BlockSpec(shape, lambda g: (0,) * len(shape), pipeline_mode=pl.Buffered(1))

    shape = jax.ShapeDtypeStruct
    if talks:
        got = [shape(array.shape, array.dtype) for array in (biases, others[0], w, *others[1:])]
        small = got[: HEADS + 1]
        got_specs = [held(*array.shape) for array in small] + [anywhere] * (len(others) - 1)
        other_specs = [held(*others[0].shape)] + [anywhere] * (len(others) - 1)
        landing = [pltpu.VMEM(array.shape, array.dtype) for array in small]
        talk = [pltpu.SemaphoreType.DMA((12,)), pltpu.SemaphoreType.DMA((12,))]
        params = pltpu.CompilerParams(vmem_limit_bytes=56 * MIB, collective_id=1, has_side_effects=True)
    else:
        got, got_specs, landing, talk = [], [], [], []
        other_specs = [held(*array.shape) for array in others]
        params = pltpu.CompilerParams(vmem_limit_bytes=56 * MIB)
    return pl.pallas_call(
        functools.partial(attend_forward_kernel, talks),
        grid=(pairs,),
        in_specs=[column_blocks(), held(*w.shape), held(*biases.shape), held(CROWS, CCOLS, PAIR), other_specs],
        out_specs=[
            pl.BlockSpec((2, 3, CROWS, CCOLS, PAIR), lambda g: (g // 2, 0, 0, 0, 0)),
            pl.BlockSpec((CROWS, CCOLS, PAIR), lambda g: (0, 0, g)),
            pl.BlockSpec((None, 12, 8, 2 * LATE), lambda g: (g, 0, 0, 0)),
            anywhere,
            anywhere,
            got_specs,
        ],
        out_shape=[
            shape((pairs, 3, CROWS, CCOLS, PAIR), bf16),
            shape((CROWS, CCOLS, pairs * PAIR), bf16),
            shape((pairs, 12, 8, 2 * LATE), f32),
            shape((pairs, CROWS // QROWS, LATE // PAIR, ROWS_EARLY, PAIR), bf16),
            shape((pairs, CROWS // QROWS, LATE // PAIR, ROWS_LATE, PAIR), bf16),
            got,
        ],
        scratch_shapes=[
            pltpu.VMEM((HALF, 2 * QCOLS, LATE), f32),
            pltpu.VMEM(w.shape, bf16),
            pltpu.VMEM(biases.shape, f32),
            pltpu.VMEM((2, 2, LATE // PAIR, ROWS_EARLY, PAIR), bf16),
            pltpu.VMEM((2, 2, LATE // PAIR, ROWS_LATE, PAIR), bf16),
            pltpu.VMEM((12 * COLS[0][2], LATE), f32),
            pltpu.VMEM((16 * COLS[0][2], LATE), f32),
            pltpu.SemaphoreType.DMA((2, 2)),
            landing,
            talk,
        ],
        compiler_params=params,
        cost_estimate=pl.CostEstimate(flops=24_000_000_000, bytes_accessed=60 * MIB, transcendentals=16_000_000),
        name="attend_forward",
    )([x] * (D // PAIR), w, biases, hot, others)


class Links:
    def __init__(self, send, recv):
        self.me, self.place = lax.axis_index("dp"), lax.axis_index("mp")
        self.send, self.recv, self.used = send, recv, 0

    def across(self):
        return self.me, 1 - self.place

    def numbers(self, count):
        self.used += count
        return self.used - count

    def copy(self, source, target, number, to):
        return pltpu.make_async_remote_copy(
            src_ref=source,
            dst_ref=target,
            send_sem=self.send.at[number],
            recv_sem=self.recv.at[number],
            device_id=to,
            device_id_type=pl.DeviceIdType.MESH,
        )

    def meet(self, others):
        barrier = pltpu.get_barrier_semaphore()
        for other in others:
            pl.semaphore_signal(barrier, inc=1, device_id=other, device_id_type=pl.DeviceIdType.MESH)
        pl.semaphore_wait(barrier, len(others))


class Levels:
    def __init__(self, links, groups):
        self.links, self.groups = links, groups

    def __len__(self):
        return len(self.groups)

    def parts(self, level):
        return 1 << len(self.groups[level])

    def index(self, device, level):
        return lax.rem(device // (1 << self.groups[level][0]), self.parts(level))

    def near(self, level):
        me, found = self.links.me, []
        for k in range(1, self.parts(level)):
            to = me
            for n, b in enumerate(self.groups[level]):
                if k >> n & 1:
                    to = to + (1 << b) * (1 - 2 * lax.rem(me // (1 << b), 2))
            found.append((k - 1, (to, self.links.place)))
        return found

    def owned(self, rows, level):
        start, size = 0, rows
        for k in range(level):
            size //= self.parts(k)
            start = start + self.index(self.links.me, k) * size
        return start, size

    def shares(self, rows, level):
        start, size = self.owned(rows, level)
        size //= self.parts(level)
        away = [start + self.index(to, level) * size for _, (to, _) in self.near(level)]
        return start + self.index(self.links.me, level) * size, away, size


def rows_at(ref, start, size):
    return ref.at[pl.ds(pl.multiple_of(start, 16), size)]


def add_rows(target, first, others, step):
    @pl.loop(0, target.shape[0] // step)
    def _(k):
        rows = pl.ds(pl.multiple_of(k * step, 16), step)
        total = first[rows].astype(f32)
        for other in others:
            total = total + other[rows].astype(f32)
        target[rows] = total.astype(target.dtype)


def add_small(running, arrived):
    terms = [running[...]] + arrived
    while len(terms) > 1:
        terms = [terms[k] + terms[k + 1] for k in range(0, len(terms), 2)]
    running[...] = terms[0]


class FeedSum:
    def __init__(self, links, levels, before, work, work_other, full, parts, parts_other, part_cross, tiny=None):
        self.links, self.levels, self.before = links, levels, before
        self.works, self.full = (work, work_other), full
        self.parts, self.part_cross = (parts, parts_other), part_cross
        self.rows = work.shape[0]
        self.tiny = tiny
        downs = [("down", level) for level in range(len(levels))]
        ups = [("up", level) for level in reversed(range(len(levels)))]
        self.stages = downs[:before] + [("cross", 0)] + downs[before:] + ups
        self.last = len(self.stages)
        self.base = [links.numbers(3 * levels.parts(level)) for _, level in self.stages]

    def copies(self, stage):
        links, levels, base = self.links, self.levels, self.base[stage]
        kind, level = self.stages[stage]
        near = levels.near(level)
        if kind == "up":
            mine = rows_at(self.full, *levels.owned(self.rows, level + 1))
            return [links.copy(mine, mine, base + k, to) for k, to in near]
        if kind == "cross":
            near = [(0, links.across())]
            kept = rows_at(self.works[1], *levels.owned(self.rows, self.before))
            made = [links.copy(kept, self.part_cross, base, links.across())]
        else:
            made = self.shared(stage, 1 if level < self.before else 0)
        if self.tiny:
            number = base + 2 * levels.parts(level)
            _, running, arrived = self.tiny
            made += [links.copy(running, arrived.at[stage, k], number + k, to) for k, to in near]
        return made

    def shared(self, stage, side):
        levels, base, level = self.levels, self.base[stage], self.stages[stage][1]
        _, away, size = levels.shares(self.rows, level)
        source = self.works[side]
        made = []
        for k, to in levels.near(level):
            number, part = base + side * levels.parts(level) + k, self.parts[side][level].at[k]
            made.append(self.links.copy(rows_at(source, away[k], size), part, number, to))
        return made

    def gather(self, stage, side):
        levels, level = self.levels, self.stages[stage][1]
        kept, _, size = levels.shares(self.rows, level)
        source = rows_at(self.works[side], kept, size)
        target = rows_at(self.full if level == len(levels) - 1 else self.works[side], kept, size)
        parts = [self.parts[side][level].at[k] for k, _ in levels.near(level)]
        add_rows(target, source, parts, levels.owned(self.rows, len(levels))[1])

    def finish(self, stage):
        levels = self.levels
        kind, level = self.stages[stage]
        for copy in self.copies(stage):
            copy.wait()
        unit = levels.owned(self.rows, len(levels))[1]
        if kind == "cross":
            mine = rows_at(self.works[0], *levels.owned(self.rows, self.before))
            add_rows(mine, mine, [self.part_cross], unit)
        elif kind == "down":
            self.gather(stage, 1 if level < self.before else 0)
        if self.tiny and kind != "up":
            _, running, arrived = self.tiny
            if kind == "cross":
                running[0:8] += arrived[stage, 0, 0:8]
                running[8:10] += arrived[stage, 0, 10:12]
            else:
                add_small(running, [arrived[stage, k] for k, _ in levels.near(level)])

    def step(self, stage):
        if 2 <= stage <= self.before + 1:
            for copy in self.shared(stage - 2, 0):
                copy.wait()
            self.gather(stage - 2, 0)
        if stage > 0:
            self.finish(stage - 1)
        elif self.tiny:
            self.tiny[1][...] = self.tiny[0][...]
        if stage < self.last:
            for copy in self.copies(stage):
                copy.start()
        if 1 <= stage <= self.before:
            for copy in self.shared(stage - 1, 0):
                copy.start()


class HeadSum:
    def __init__(self, links, levels, away, arrived, work, full, parts, bias_away, bias_arrived, bias, bias_parts):
        self.links, self.levels = links, levels
        self.away, self.arrived, self.work, self.full, self.parts = away, arrived, work, full, parts
        self.bias_away, self.bias_arrived, self.bias, self.bias_parts = bias_away, bias_arrived, bias, bias_parts
        self.rows = work.shape[0]
        self.cross_base = links.numbers(2)
        self.last = 2 * len(levels)
        self.base = [links.numbers(2 * levels.parts(self.level(stage))) for stage in range(self.last)]

    def level(self, stage):
        return min(stage, self.last - 1 - stage)

    def cross(self):
        to = self.links.across()
        return [
            self.links.copy(self.away, self.arrived, self.cross_base, to),
            self.links.copy(self.bias_away, self.bias_arrived, self.cross_base + 1, to),
        ]

    def arriving(self, level, k):
        first, size = 0, self.rows
        for at in range(level):
            size //= self.levels.parts(at)
            first += size * (self.levels.parts(at) - 1)
        size //= self.levels.parts(level)
        return self.parts.at[first + k * size : first + (k + 1) * size]

    def copies(self, stage):
        links, levels, base, level = self.links, self.levels, self.base[stage], self.level(stage)
        near = levels.near(level)
        if stage >= len(levels):
            mine = rows_at(self.full, *levels.owned(self.rows, level + 1))
            return [links.copy(mine, mine, base + k, to) for k, to in near]
        _, away, size = levels.shares(self.rows, level)
        return [
            links.copy(rows_at(self.work, away[k], size), self.arriving(level, k), base + k, to) for k, to in near
        ] + [links.copy(self.bias, self.bias_parts.at[level, k], base + levels.parts(level) + k, to) for k, to in near]

    def step(self, stage):
        levels = self.levels
        unit = levels.owned(self.rows, len(levels))[1]
        for copy in self.cross() if stage == 0 else self.copies(stage - 1):
            copy.wait()
        if stage == 0:
            add_rows(self.work, self.work, [self.arrived], unit)
            self.bias[...] += self.bias_arrived[...]
        elif stage <= len(levels):
            level = stage - 1
            kept, _, size = levels.shares(self.rows, level)
            source = rows_at(self.work, kept, size)
            target = rows_at(self.full, kept, size) if stage == len(levels) else source
            add_rows(target, source, [self.arriving(level, k) for k, _ in levels.near(level)], unit)
            add_small(self.bias, [self.bias_parts[level, k] for k, _ in levels.near(level)])
        if stage < self.last:
            for copy in self.copies(stage):
                copy.start()


def groups_of(dp):
    bits = list(range(dp.bit_length() - 1))
    return [bits[:1], bits[1:2], bits[2:]], [bits[:1], bits[1:]]


PLAN = {
    (0, 1): [("expand", 1), ("reduce", 1)],
    (1, 1): [("reduce", 2), ("expand", 2)],
    (1, 3): [("reduce", 3)],
    (1, 4): [("expand", 3), (0, "cross")],
    (2, 1): [("reduce", 4), (1, "cross")],
    (2, 3): [("expand", 4)],
    (2, 4): [(0, 0), ("reduce", 5)],
    (3, 1): [(0, 1)],
    (3, 2): [("expand", 5), ("reduce", 6)],
    (3, 3): [(0, 2)],
    (3, 4): [(1, 0), ("reduce", 7)],
    (4, 1): [(1, 1), ("expand", 6)],
    (4, 2): [(0, 3)],
    (4, 3): [(1, 2), ("expand", 7)],
    (4, 4): [(0, 4), (1, 3), (1, 4)],
}


def attend_backward_kernel(
    dp, qkv_ref, go_ref, delta_ref, rate_ref, x_hbm, w_hbms, gone_hbm, early_hbm, late_hbm, feeds, merges, tiny_ref,
    gx_hbm, gw_ref, gb_ref, sums_out, gk_ref, gv_ref, gqkv_all, early_ref, late_ref, gx_ref, x_ref, w_ref, sems, talk,
):
    pairs = pl.num_programs(0) - 1
    step = pl.program_id(0)
    pair = lax.rem(step + pairs // 2, pairs)
    if dp:
        expand_out, reduce_out, merge_out, small_out, hidden_out = sums_out
        turned_ref, *talk = talk
        expand, reduce, heads, (small, small_in), (send, recv) = talk
        links = Links(send, recv)
        feed_levels, pair_levels = (Levels(links, groups) for groups in groups_of(dp))
        sums = {
            "expand": FeedSum(links, feed_levels, 1, *expand, tiny=(tiny_ref, small, small_in)),
            "reduce": FeedSum(links, feed_levels, 2, *reduce),
        }
        for number in range(2):
            sums[number] = HeadSum(links, pair_levels, *heads[number])

    def act(what, stage):
        if stage == "cross":
            for copy in sums[what].cross():
                copy.start()
        else:
            sums[what].step(stage)
            if what == "expand" and stage == sums[what].last:
                leave["expand"].start()
                small_out[...] = small[0:8]
                hidden_out[...] = jnp.concatenate([small[8:9], small[9:10]], axis=1)
            if what == "reduce" and stage == sums[what].last:
                for at in range(0, FF // 2, D):
                    turned_ref[at : at + D] = sums[what].full[:, at : at + D].T
                leave["reduce"].start()

    def event(at_step, place):
        if not dp or (at_step, place) not in PLAN:
            return

        @pl.when(step == at_step)
        def _():
            for what, stage in PLAN[at_step, place]:
                act(what, stage)

    def stored(of, half):
        rows = pl.ds(2 * half, 2)
        return [
            pltpu.make_async_copy(early_hbm.at[of, rows], early_ref.at[half], sems.at[half, 0]),
            pltpu.make_async_copy(late_hbm.at[of, rows], late_ref.at[half], sems.at[half, 1]),
        ]

    fill = pltpu.make_async_copy(gone_hbm, gx_ref, sems.at[2, 0])
    x_in = [
        pltpu.make_async_copy(x_hbm.at[:, :, pl.ds(k * PAIR, PAIR)], x_ref.at[k], sems.at[3 + k, 0])
        for k in range(D // PAIR)
    ]
    w_in = [pltpu.make_async_copy(w_hbms[k], w_ref.at[k], sems.at[3 + k, 1]) for k in range(2)]
    gx_out = [
        pltpu.make_async_copy(gx_ref.at[pl.ds(k * 8, 8)], gx_hbm.at[pl.ds(k * 8, 8)], sems.at[7 + k, 0])
        for k in range(4)
    ]
    if dp:
        feeds_in = [
            pltpu.make_async_copy(feeds[n][side], sums[name].works[side], sems.at[11 + n, side])
            for n, name in enumerate(("expand", "reduce"))
            for side in range(2)
        ]
        leave = {
            "expand": pltpu.make_async_copy(sums["expand"].full, expand_out, sems.at[7, 1]),
            "reduce": pltpu.make_async_copy(turned_ref, reduce_out, sems.at[8, 1]),
        }

    @pl.when(step == 0)
    def _():
        for copy in stored(pair, 0):
            copy.start()
        if dp:
            for copy in feeds_in:
                copy.start()
            links.meet([links.across()] + [to for level in range(2) for _, to in pair_levels.near(level)])
            for copy in feeds_in:
                copy.wait()
            for name in ("expand", "reduce"):
                sums[name].step(0)

    def fetch(half):
        if half == 0:
            for copy in stored(pair, 1):
                copy.start()
        else:

            @pl.when(step < pairs - 1)
            def _():
                for copy in stored(lax.rem(step + 1 + pairs // 2, pairs), 0):
                    copy.start()

        for copy in stored(pair, half):
            copy.wait()

        @pl.when(step == half)
        def _():
            for copy in [*w_in, fill] if half else x_in:
                copy.start()

    @pl.when(step < pairs)
    def _():
        attend_backward_pair(
            pair, qkv_ref, go_ref, delta_ref, rate_ref, gqkv_all.at[pair], early_ref, late_ref, gk_ref, gv_ref, fetch,
            lambda slot: [event(k, slot) for k in range(4)],
        )
        grad = jnp.concatenate([gqkv_all[pair, part].reshape(POS, PAIR) for part in range(3)], axis=1)

        @pl.when(step == 0)
        def _():
            for copy in x_in:
                copy.wait()

        x_all = jnp.concatenate([x_ref[k].reshape(POS, PAIR) for k in range(D // PAIR)], axis=1)
        grad_weights = dot_tn(grad, x_all).T.astype(bf16)
        grad_bias = jnp.broadcast_to(jnp.sum(grad.astype(f32), axis=0, keepdims=True), (8, 3 * PAIR))
        if not dp:
            gw_ref[...] = grad_weights
            gb_ref[...] = grad_bias
        else:
            for number in range(2):
                one = sums[number]
                for first, ref, small_ref in ((0, one.away, one.bias_away), (2, one.work, one.bias)):

                    @pl.when(step == first + number)
                    def _():
                        ref[:, 0 : 3 * PAIR] = grad_weights
                        small_ref[...] = grad_bias
                        if number == 0:
                            merge = merges[1 if first == 0 else 0]
                            for k in range(2):
                                span = slice(k * (D // 2), (k + 1) * (D // 2))
                                ref[span, 3 * PAIR :] = merge[:, span]

            for k in range(4):
                event(k, 4)

    @pl.when(step == pairs)
    def _():
        for copy in [fill, *w_in]:
            copy.wait()
        weights = jnp.concatenate(
            [
                w_ref[p // 2, part, :, p % 2 * PAIR : (p % 2 + 1) * PAIR]
                for p in range(D // PAIR)
                for part in range(3)
            ],
            axis=1,
        )
        for part in range(4):
            event(4, part)
            rows = slice(part * 8, part * 8 + 8)
            grads = [gqkv_all[p, k, rows].reshape(8 * CCOLS, PAIR) for p in range(D // PAIR) for k in range(3)]
            product = dot_nt(jnp.concatenate(grads, axis=1), weights).reshape(8, CCOLS, D)
            gx_ref[rows] = (gx_ref[rows].astype(f32) + product).astype(bf16)
            gx_out[part].start()
        event(4, 4)
        if dp:
            for number in range(2):
                for part in range(3):
                    lanes = slice(part * PAIR, (part + 1) * PAIR)
                    gw_ref[part, :, number * PAIR : (number + 1) * PAIR] = sums[number].full[:, lanes]
            for k in range(2):
                span = slice(k * (D // 2), (k + 1) * (D // 2))
                merge_out[:, span] = sums[0].full[span, 3 * PAIR :]
            for row, part in enumerate((0, 2)):
                lanes = slice(part * PAIR, (part + 1) * PAIR)
                gb_ref[row : row + 1] = jnp.concatenate([sums[p].bias[0:1, lanes] for p in range(2)], axis=1)
            for copy in leave.values():
                copy.wait()
        for copy in gx_out:
            copy.wait()


def attend_backward_pair(
    pair, qkv_ref, go_ref, delta_ref, rate_ref, gqkv_ref, early_ref, late_ref, gk_ref, gv_ref, fetch, event
):
    gk_ref[...] = jnp.zeros_like(gk_ref)
    gv_ref[...] = jnp.zeros_like(gv_ref)

    def gap(i, j):
        q0, c0, width = COLS[j]
        q_rows = query_rows(i)
        grads = go_ref[q_rows, q0 : q0 + QCOLS, :].reshape(QB, PAIR)
        deltas = delta_ref[q_rows, q0 : q0 + QCOLS, :].reshape(QB, PAIR)
        values = window(qkv_ref.at[2], i, c0, width)
        ones = jnp.broadcast_to(lane_row(0, 24), values.shape)
        values = jnp.concatenate([values, ones], axis=1)
        size = values.shape[0] - HALF * width
        own_grad = stacked(*(own_lanes(grads, head) for head in range(2)))
        own_delta = stacked(*(deltas * lane_row(3 * (2 * pair + head), 3) for head in range(2)))
        sides = jnp.concatenate([own_grad, own_delta], axis=1)
        return dot_nt(values[:size], sides[:LATE]), dot_nt(values, sides[LATE:]), own_grad

    def block(i, j, gaps, gaps_late, own_grad):
        q0, c0, width = COLS[j]
        q_rows = query_rows(i)
        queries = qkv_ref[0, q_rows, q0 : q0 + QCOLS, :].reshape(QB, PAIR)
        own = stacked(*(own_lanes(queries, head, 0.125) for head in range(2)))
        keys = window(qkv_ref.at[1], i, c0, width)
        count = keys.shape[0]
        size = count - HALF * width
        rate = rate_ref[i * 3 + j, 0:1, :].astype(bf16)
        chances = get_tiles(early_ref.at[i // 2, i % 2], AT_EARLY[j], size) * rate[:, :LATE]
        late = get_tiles(late_ref.at[i // 2, i % 2], AT_LATE[j], count) * rate[:, LATE:]
        slopes = chances * gaps.astype(bf16)
        slopes_late = late * gaps_late.astype(bf16)
        both = jnp.concatenate([slopes, slopes_late[:size]], axis=1)
        out = dot_tn(both, keys[:size])
        out_late = out[LATE:] + dot_tn(slopes_late[size:], keys[size:])
        half = LATE // 2
        out = [jnp.where(lanes_of(part[:half]) < HD, part[:half], part[half:]) for part in (out[:LATE], out_late)]
        out = (jnp.concatenate(out, axis=0) * 0.125).astype(bf16)
        gqkv_ref[0, q_rows, q0 : q0 + QCOLS, :] = out.reshape(QROWS, QCOLS, PAIR)
        rows = key_rows(i)
        for ref, early, later, side in ((gk_ref, slopes, slopes_late, own), (gv_ref, chances, late, own_grad)):
            both = jnp.concatenate([early, later[:size]], axis=1)
            part = jnp.concatenate([dot(both, side), dot(later[size:], side[LATE:])], axis=0)
            ref[rows, c0 : c0 + width, :] += part.reshape(-1, width, PAIR)

    order = [(i, j) for i in range(CROWS // QROWS) for j in range(3)]
    ready = gap(*order[0])
    for n, (i, j) in enumerate(order):
        now = ready
        if n + 1 < len(order):
            ready = gap(*order[n + 1])
        if j == 0 and i % 2 == 0:
            fetch(i // 2)
        block(i, j, *now)
        if j == 2:
            event(i)

    gqkv_ref[1] = gk_ref[...].astype(bf16)
    gqkv_ref[2] = gv_ref[...].astype(bf16)


def attend_backward(qkv, grad_att, delta, rate, x, w_halves, grad_one, a_stored, b_stored, feeds, merges, tiny, dp):
    pairs = D // PAIR
    levels, pair_levels = ([1 << len(group) for group in groups] for groups in groups_of(max(dp, 1)))

    def turn(g):
        return lax.rem(jnp.minimum(g, pairs - 1) + pairs // 2, pairs)

    def held(*shape):
        return pl.BlockSpec(shape, lambda g: (0,) * len(shape), pipeline_mode=pl.Buffered(1))

    shape, vmem = jax.ShapeDtypeStruct, pltpu.VMEM
    anywhere = pl.BlockSpec(memory_space=pl.ANY)
    outs = [((CROWS, CCOLS, D), bf16)]
    if dp:
        wide = FF // 2
        feed_specs, merge_specs, tiny_spec = [[anywhere] * 2] * 2, [held(D // 2, D)] * 2, held(16, D)
        sum_outs = [((D, wide), bf16), ((wide, D), bf16), ((D // 2, D), bf16), ((8, D), f32), ((1, wide), f32)]
        sum_specs = [anywhere, anywhere] + [held(*dims) for dims, _ in sum_outs[2:]]
        outs += [((3, D, 2 * PAIR), bf16), ((2, 2 * PAIR), f32)]
        out_specs = [anywhere] + [held(*dims) for dims, _ in outs[1:]]
        copies = 2 * 3 * (2 * sum(levels) + max(levels)) + 2 * (2 + 4 * sum(pair_levels))

        def feed_scratch(before):
            parts, size = [], D
            for level in levels:
                size //= level
                parts.append(vmem((level - 1, size, wide), bf16))
            crossing = D
            for level in levels[:before]:
                crossing //= level
            return [vmem((D, wide), bf16)] * 3 + [parts, parts[:before], vmem((crossing, wide), bf16)]

        talk = [
            vmem((wide, D), bf16),
            feed_scratch(1),
            feed_scratch(2),
            [
                [vmem((D, width), bf16)] * 5
                + [vmem((8, 3 * PAIR), f32)] * 3
                + [vmem((len(pair_levels), max(pair_levels) - 1, 8, 3 * PAIR), f32)]
                for width in (3 * PAIR + D // 2, 3 * PAIR)
            ],
            [vmem((16, D), f32), vmem((len(levels) + 1, max(levels) - 1, 16, D), f32)],
            [pltpu.SemaphoreType.DMA((copies,)), pltpu.SemaphoreType.DMA((copies,))],
        ]
        params = pltpu.CompilerParams(vmem_limit_bytes=63 * MIB, collective_id=0, has_side_effects=True)
    else:
        feeds, merges, tiny, feed_specs, merge_specs, tiny_spec, sum_outs, sum_specs, talk = ([] for _ in range(9))
        outs += [((pairs, D, 3 * PAIR), bf16), ((pairs, 8, 3 * PAIR), f32)]
        out_specs = [
            anywhere,
            pl.BlockSpec((None, D, 3 * PAIR), lambda g: (turn(g), 0, 0)),
            pl.BlockSpec((None, 8, 3 * PAIR), lambda g: (turn(g), 0, 0)),
        ]
        params = pltpu.CompilerParams(vmem_limit_bytes=60 * MIB)
    return pl.pallas_call(
        functools.partial(attend_backward_kernel, dp),
        grid=(pairs + 1,),
        in_specs=[
            pl.BlockSpec((None, 3, CROWS, CCOLS, PAIR), lambda g: (turn(g), 0, 0, 0, 0)),
            pl.BlockSpec((CROWS, CCOLS, PAIR), lambda g: (0, 0, turn(g))),
            held(CROWS, CCOLS, PAIR),
            pl.BlockSpec((None, 12, 8, 2 * LATE), lambda g: (turn(g), 0, 0, 0)),
            anywhere,
            [anywhere] * 2,
            anywhere, anywhere, anywhere,
            feed_specs,
            merge_specs,
            tiny_spec,
        ],
        out_specs=[*out_specs, sum_specs],
        out_shape=[shape(*out) for out in outs] + [[shape(*out) for out in sum_outs]],
        scratch_shapes=[
            vmem((CROWS, CCOLS, PAIR), f32),
            vmem((CROWS, CCOLS, PAIR), f32),
            vmem((pairs, 3, CROWS, CCOLS, PAIR), bf16),
            vmem((2, 2, LATE // PAIR, ROWS_EARLY, PAIR), bf16),
            vmem((2, 2, LATE // PAIR, ROWS_LATE, PAIR), bf16),
            vmem((CROWS, CCOLS, D), bf16),
            vmem((D // PAIR, CROWS, CCOLS, PAIR), bf16),
            vmem((2, 3, D, 2 * PAIR), bf16),
            pltpu.SemaphoreType.DMA((13, 2)),
            talk,
        ],
        compiler_params=params,
        cost_estimate=pl.CostEstimate(flops=50_000_000_000, bytes_accessed=90 * MIB, transcendentals=0),
        name="attend_backward",
    )(qkv, grad_att, delta, rate, x, w_halves, grad_one, a_stored, b_stored, feeds, merges, tiny)


ROWS = 512
CHUNK = 512


def feed_kernel(
    x_ref, ct_ref, att_ref, wm_refs, we_refs, be_refs, wr_refs, vec_refs,
    out_ref, gone_ref, gatt_ref, delta_ref, expand_refs, reduce_refs, merge_refs, tiny_ref,
    hid_ref, slope_ref, gpre_ref, grad_rows_t, acc_m, acc_e, acc_r, acc_be, acc_vec, choose_ref, kind_ref,
):
    step = pl.program_id(0)
    last = pl.num_programs(0) - 1
    slot = lax.rem(step, 2)

    @pl.when(step == 0)
    def _():
        for ref in (hid_ref, grad_rows_t, acc_m, acc_e, acc_r, acc_be, acc_vec):
            ref[...] = jnp.zeros_like(ref)
        lane = lax.broadcasted_iota(jnp.int32, (D, PAIR), 1)
        head = lax.broadcasted_iota(jnp.int32, (D, PAIR), 0) // HD
        choose_ref[...] = jnp.where(head == lane // 3, -1.0, 0.0).astype(bf16)
        kind_ref[...] = jnp.where(lane[0:8] % 3 == lax.broadcasted_iota(jnp.int32, (8, PAIR), 0), 1.0, 0.0)

    b_merge, gain_one, shift_one, b_reduce, gain_two, shift_two = (ref[...] for ref in vec_refs)
    half = D // 2
    chunks = [(side, at) for side in range(2) for at in range(0, FF // 2, CHUNK)]
    spans = [slice(n * CHUNK, (n + 1) * CHUNK) for n in range(len(chunks))]

    def normal(z):
        centred = z - jnp.mean(z, axis=1, keepdims=True)
        rate = lax.rsqrt(jnp.mean(centred * centred, axis=1, keepdims=True) + 1e-5)
        return centred * rate, rate

    def normal_back(grad, normed, rate):
        mean = jnp.mean(grad, axis=1, keepdims=True)
        slant = jnp.mean(grad * normed, axis=1, keepdims=True)
        return rate * (grad - mean - normed * slant)

    def column_sum(z):
        return jnp.sum(z, axis=0, keepdims=True)

    def eights(z):
        return sum(z[at : at + 8] for at in range(0, z.shape[0], 8))


    def weight_reduce(n):
        acc_r[:, spans[n]] += dot(grad_rows_t[...], hid_ref[1 - slot, :, spans[n]])

    def norm_one(x, branch):
        first, rate = normal(x.astype(f32) + b_merge + branch)
        normed = first * gain_one + shift_one
        return first, rate, normed, normed.astype(bf16)

    def norm_two(z, cotangent):
        second, rate = normal(z)
        cotangent = cotangent.astype(f32)
        grad = normal_back(cotangent * gain_two, second, rate)
        out = (second * gain_two + shift_two).astype(bf16)
        return out, grad, grad.astype(bf16), eights(cotangent * second), eights(cotangent), eights(grad)

    def back_one(grad_normed, first, rate):
        grad = normal_back(grad_normed * gain_one, first, rate)
        return grad.astype(bf16), eights(grad_normed * first), eights(grad_normed), eights(grad)

    def gelu(pre):
        square = pre * pre
        bent = jnp.tanh(pre * (GC + (GC * GA) * square))
        lead = 0.5 + 0.5 * bent
        hidden = pre * lead
        slope = lead + (hidden * (1.0 - bent)) * (GC + (3 * GC * GA) * square)
        return hidden.astype(bf16), slope.astype(bf16)

    def back(grad, slope):
        grad = (grad * slope.astype(f32)).astype(bf16)
        return grad, eights(grad.astype(f32))

    def expand(rows_in, n):
        side, at = chunks[n]
        return dot(rows_in, we_refs[side][:, at : at + CHUNK]) + be_refs[side][0:1, at : at + CHUNK]

    def grad_hidden(grad_rows, n):
        side, at = chunks[n]
        return dot_nt(grad_rows, wr_refs[side][at : at + CHUNK, :])

    @pl.when(step == last)
    def _():
        for n in range(len(chunks)):
            weight_reduce(n)
        for side in range(2):
            span = slice(side * (FF // 2), (side + 1) * (FF // 2))
            expand_refs[side][...] = acc_e[:, span].astype(bf16)
            reduce_refs[side][...] = acc_r[:, span].astype(bf16)
            merge_refs[side][...] = acc_m[side * half : (side + 1) * half].astype(bf16)
        tiny_ref[...] = jnp.zeros_like(tiny_ref)
        tiny_ref[0:8] = acc_vec[...]
        for k in range(FF // D):
            tiny_ref[8 + k : 9 + k] = acc_be[:, k * D : (k + 1) * D]

    @pl.when(step < last)
    def _():
        branch_one = dot(att_ref[:, :half], wm_refs[0][...]) + dot(att_ref[:, half:], wm_refs[1][...])
        for n in range(len(chunks) // 2):
            weight_reduce(n)
        first, rate_one, normed_one, rows_in = sliced(norm_one, 32, x_ref[...], branch_one)
        summed_two = normed_one + b_reduce
        ready = expand(rows_in, 0)
        for n, (side, at) in enumerate(chunks):
            now = ready
            if n + 1 < len(chunks):
                ready = expand(rows_in, n + 1)
            hidden, slope = sliced(gelu, 16, now)
            hid_ref[slot, :, spans[n]] = hidden
            slope_ref[:, spans[n]] = slope
            summed_two += dot(hidden, wr_refs[side][at : at + CHUNK, :])
        for n in range(len(chunks) // 2, len(chunks)):
            weight_reduce(n)
        out_ref[...], grad_two, grad_rows, *partial = sliced(norm_two, 32, summed_two, ct_ref[...])
        for k, part in zip((4, 5, 3), partial):
            acc_vec[k : k + 1] += column_sum(part)
        grad_rows_t[...] = grad_rows.T
        grad_normed = grad_two
        ready = grad_hidden(grad_rows, 0)
        for n, (side, at) in enumerate(chunks):
            now = ready
            if n + 1 < len(chunks):
                ready = grad_hidden(grad_rows, n + 1)
            grad_pre, part = sliced(back, 32, now, slope_ref[:, spans[n]])
            gpre_ref[:, spans[n]] = grad_pre
            acc_be[:, spans[n]] += column_sum(part)
            grad_normed += dot_nt(grad_pre, we_refs[side][:, at : at + CHUNK])
        rows_t = rows_in.T
        for n in range(len(chunks)):
            acc_e[:, spans[n]] += dot(rows_t, gpre_ref[:, spans[n]])
        grad_one_rows, *partial = sliced(back_one, 32, grad_normed, first, rate_one)
        gone_ref[...] = grad_one_rows
        for k, part in zip((1, 2, 0), partial):
            acc_vec[k : k + 1] += column_sum(part)
        for side in range(2):
            gatt_ref[:, side * half : (side + 1) * half] = dot_nt(grad_one_rows, wm_refs[side][...]).astype(bf16)
        acc_m[...] += dot(att_ref[...].T, grad_one_rows)
        products = gatt_ref[...].astype(f32) * att_ref[...].astype(f32)
        deltas = three_parts(dot(products.astype(bf16), choose_ref[...]))
        delta_ref[...] = sum(part * kind_ref[k : k + 1] for k, part in enumerate(deltas)).astype(bf16)


def feed(x, cotangent, att, wms, wes, be, wrs, vecs):
    half = D // 2

    def rows(width):
        return pl.BlockSpec((ROWS, width), lambda s: (jnp.minimum(s, POS // ROWS - 1), 0))

    def whole(*shape):
        return pl.BlockSpec(shape, lambda s: (0, 0), pipeline_mode=pl.Buffered(1))

    def held(*shape):
        return pl.BlockSpec(shape, lambda s: (0, 0))

    shape = jax.ShapeDtypeStruct
    return pl.pallas_call(
        feed_kernel,
        grid=(POS // ROWS + 1,),
        in_specs=[
            rows(D), rows(D), rows(D), [whole(half, D)] * 2, [whole(D, FF // 2)] * 2,
            [whole(1, FF // 2)] * 2, [whole(FF // 2, D)] * 2, [whole(1, D)] * 6,
        ],
        out_specs=[
            rows(D), rows(D), rows(D), rows(PAIR), [held(D, FF // 2)] * 2, [held(D, FF // 2)] * 2, [held(half, D)] * 2,
            held(16, D),
        ],
        out_shape=[
            shape((POS, D), bf16), shape((POS, D), bf16), shape((POS, D), bf16), shape((POS, PAIR), bf16),
            [shape((D, FF // 2), bf16)] * 2, [shape((D, FF // 2), bf16)] * 2, [shape((half, D), bf16)] * 2,
            shape((16, D), f32),
        ],
        scratch_shapes=[
            pltpu.VMEM((2, ROWS, FF), bf16),
            pltpu.VMEM((ROWS, FF), bf16),
            pltpu.VMEM((ROWS, FF), bf16),
            pltpu.VMEM((D, ROWS), bf16),
            pltpu.VMEM((D, D), f32),
            pltpu.VMEM((D, FF), f32),
            pltpu.VMEM((D, FF), f32),
            pltpu.VMEM((1, FF), f32),
            pltpu.VMEM((8, D), f32),
            pltpu.VMEM((D, PAIR), bf16),
            pltpu.VMEM((8, PAIR), f32),
        ],
        compiler_params=pltpu.CompilerParams(vmem_limit_bytes=60 * MIB),
        cost_estimate=pl.CostEstimate(flops=44_000_000_000, bytes_accessed=40 * MIB, transcendentals=6_000_000),
        name="feed",
    )(x, cotangent, att, wms, wes, be, wrs, vecs)


def finish_kernel(*refs):
    count = (len(refs) - 5) // 2
    for source, target in zip(refs[: count - 1], refs[count:-6]):
        target[...] = source[...].astype(f32)
    for k, target in enumerate(refs[-6:]):
        target[...] = refs[count - 1][k : k + 1]


def finish(wide, small, vecs):
    def block(array, parts):
        dims = array.shape
        part = dims[:-2] + (dims[-2] // parts, dims[-1])
        return pl.BlockSpec(part, lambda s: (0,) * (len(dims) - 2) + ((s if parts > 1 else 0), 0))

    parts = 2
    specs = [block(array, parts) for array in wide] + [block(array, 1) for array in small]
    row = jax.ShapeDtypeStruct((1, D), f32)
    return pl.pallas_call(
        finish_kernel,
        grid=(parts,),
        in_specs=specs + [block(vecs, 1)],
        out_specs=specs + [block(row, 1)] * 6,
        out_shape=[jax.ShapeDtypeStruct(array.shape, f32) for array in (*wide, *small)] + [row] * 6,
        compiler_params=pltpu.CompilerParams(vmem_limit_bytes=63 * MIB),
        cost_estimate=pl.CostEstimate(flops=0, bytes_accessed=20 * MIB, transcendentals=0),
        name="finish",
    )(*wide, *small, vecs)


def local(
    inputs, crop_ids, w_heads, b_heads, w_merge, b_merge, gain_one, shift_one, w_expand, b_expand, w_reduce,
    b_reduce, gain_two, shift_two, cotangent, *, split,
):
    features = inputs.shape[2]
    dp, mp = split
    paired = mp == 2
    talks = paired and dp >= 8 and dp & (dp - 1) == 0 and D % (16 * dp) == 0
    place = lax.axis_index("mp")

    def both(shard, axis):
        if paired:
            return [shard, lax.ppermute(shard, "mp", [(0, 1), (1, 0)])]
        whole = lax.all_gather(shard, "mp", axis=axis, tiled=True)
        return list(jnp.split(whole, 2, axis=axis))

    def sum_parts(parts, axis):
        if paired:
            arrived = lax.ppermute(parts[1], "mp", [(0, 1), (1, 0)])
            return parts[0].astype(f32) + arrived.astype(f32)
        return lax.psum_scatter(jnp.concatenate(parts, axis=axis), "mp", scatter_dimension=axis, tiled=True)

    canvas = inputs[0].reshape(CROWS, CCOLS, features)
    labels = lax.dynamic_index_in_dim(crop_ids, place, 0, keepdims=False)
    hot = (labels[:, None] == jnp.arange(PAIR)[None, :]).astype(bf16).reshape(CROWS, CCOLS, PAIR)

    own_heads = jnp.transpose(w_heads, (1, 0, 2))
    vecs = [vec[None] for vec in (b_merge, gain_one, shift_one, b_reduce, gain_two, shift_two)]

    if talks:
        qkv, att, rate, a_stored, b_stored, got = attend_forward(
            canvas, own_heads, b_heads, hot, [b_expand[None], w_merge, w_expand, w_reduce], True
        )
        heads, merges = [own_heads, got[HEADS]], [w_merge, got[MERGE]]
        expands, reduces = [w_expand, got[EXPAND]], [w_reduce, got[REDUCE]]
        hiddens = [b_expand[None], got[HIDDEN]]
    else:
        heads, merges, expands, reduces = both(own_heads, 2), both(w_merge, 0), both(w_expand, 1), both(w_reduce, 0)
        biases = [part.astype(f32) for part in both(b_heads.astype(bf16), 1)]
        hiddens = [part[None].astype(f32) for part in both(b_expand.astype(bf16), 0)]
        qkv, att, rate, a_stored, b_stored, _ = attend_forward(
            canvas, heads[0], biases[0], hot, [heads[1], biases[1]], False
        )
    outputs, grad_one, grad_att, delta, expand_g, reduce_g, merge_g, tiny = feed(
        inputs[0], cotangent[0], att.reshape(POS, -1), merges, expands, hiddens, reduces, vecs
    )

    def canvas_of(array):
        return array.reshape(CROWS, CCOLS, -1)

    grad_inputs, heads_g, bias_g, sums = attend_backward(
        qkv, canvas_of(grad_att), canvas_of(delta), rate, canvas, heads, canvas_of(grad_one), a_stored, b_stored,
        [expand_g, reduce_g], merge_g, tiny, dp if talks else 0,
    )

    def bias_part(g_bias):
        g_bias = g_bias[:, 0].reshape(-1, 3, PAIR)
        return jnp.stack([g_bias[:, 0].reshape(-1), g_bias[:, 2].reshape(-1)])

    if talks:
        expand_g, reduce_g, merge_g, tiny_g, be_g = sums
        grad_inputs, expand_g, reduce_g, merge_g, heads_g, be_g, bias_g, *tiny_g = finish(
            [grad_inputs.reshape(POS, D), expand_g, reduce_g, merge_g, heads_g], [be_g, bias_g], tiny_g
        )
        be_g = be_g[0]
        tiny_g = [vec[0] for vec in tiny_g]
    else:
        heads_g = heads_g.reshape(-1, D, 3, PAIR).transpose(2, 1, 0, 3).reshape(3, D, -1)
        grads = (
            (jnp.split(heads_g, 2, axis=2), 2),
            (jnp.split(bias_part(bias_g).astype(bf16), 2, axis=1), 1),
            (expand_g, 1),
            ([half.T for half in reduce_g], 0),
            (merge_g, 0),
            (jnp.split(tiny[8:12].reshape(-1).astype(bf16), 2), 0),
        )
        heads_g, bias_g, expand_g, reduce_g, merge_g, be_g = (
            lax.psum(sum_parts(list(parts), axis).astype(bf16), "dp").astype(f32) for parts, axis in grads
        )
        tiny_g = lax.psum(tiny, ("dp", "mp"))
    return (
        outputs[None],
        grad_inputs.reshape(1, POS, D).astype(f32),
        jnp.transpose(heads_g.astype(f32), (1, 0, 2)),
        bias_g,
        merge_g.astype(f32),
        tiny_g[0],
        tiny_g[1],
        tiny_g[2],
        expand_g.astype(f32),
        be_g,
        reduce_g.astype(f32),
        tiny_g[3],
        tiny_g[4],
        tiny_g[5],
    )


def solution(mesh):
    rows = P(("dp", "mp"), None, None)
    weights = (P(None, None, "mp"), P(None, "mp"), P("mp", None))
    feeds = (P(None, "mp"), P("mp"), P("mp", None))
    return jax.shard_map(
        functools.partial(local, split=(mesh.shape["dp"], mesh.shape["mp"])),
        mesh=mesh,
        in_specs=(rows, P("dp", None), *weights, P(), P(), P(), *feeds, P(), P(), P(), rows),
        out_specs=(rows, rows, *weights, P(), P(), P(), *feeds, P(), P(), P()),
        check_vma=False,
    )
```
